128 devices in a mesh: gx: 8 (over x, core), gy: 4 (over z), gz: 4 (over y).
Axes of the slice: x: 4, y: 4, z: 4, core: 2. Of those that a mesh axis runs over, the one named last changes fastest.
Arguments:
- right_side: float32 [2048, 128], P(('gx', 'gy', 'gz')), may hold values from -53 to 53
- diagonal: float32 [2048, 128], P(('gx', 'gy', 'gz')), may hold values from 0.5 to 2
- near_blocks: bfloat16 [24576, 128, 128], P(('gx', 'gy', 'gz')), may hold values from -0.109375 to 0.109375
- near_rows: int32 [24576], P(('gx', 'gy', 'gz')), may hold values from 0 to 2047, as said below
- near_cols: int32 [24576], P(('gx', 'gy', 'gz')), may hold values from 0 to 2047, as said below
- near_count: int32 [128], P(('gx', 'gy', 'gz')), may hold values from 16 to 192, as said below
- basis: bfloat16 [2048, 32, 128], P(('gx', 'gy', 'gz')), may hold values from -0.5 to 0.5
- coupling: bfloat16 [65536, 1024], P(('gx', 'gy', 'gz')), may hold values from -0.41992188 to 0.41992188
- far_rows: int32 [65536], P(('gx', 'gy', 'gz')), may hold values from 0 to 2047, as said below
- far_cols: int32 [65536], P(('gx', 'gy', 'gz')), may hold values from 0 to 2047, as said below
- far_rank: int32 [65536], P(('gx', 'gy', 'gz')), may hold values from 4 to 32, as said below
Outputs:
- solution: float32 [2048, 128], P(('gx', 'gy', 'gz'))
- residual: float32 [2048, 128], P(('gx', 'gy', 'gz'))
The draws below stay inside these ranges and needn't reach their ends.
Inputs may be any that keep to these rules, and one draw needn't show every extreme that they name: `near_rows`: each slot names a cluster of the device that holds the slot, device g holding clusters g * 16 to g * 16 + 15; the first 16 slots of a device name its clusters in order. `near_cols`: each slot names a cluster of the device that holds it or of the device just before or after it in the order of gx, gy, gz; the first 16 slots of a device repeat their row cluster. `near_count`: slots at or after a device's count are unused; some device uses all 192. `far_rows`: each slot names a cluster of the device that holds the slot. `far_cols`: of the slots of one device, at most 8 name clusters of any one device, and on every device exactly 8 name clusters of some one device. `far_rank`: the first slot of every device has rank 32.
All inputs are finite; a program needn't handle non-finite values.
Results may differ from the reference program's by a relative error of at most 0.0023.
Values may be sent and summed in bfloat16 or wider, within the bound.
A program may use at most 128 MiB of HBM per device.

```python
import math
import jax
import jax.numpy as jnp
from jax import lax

M = 128
R = 32
CL = 16
NEAR_PER = 12
ITERS = 3
GROUPS = 128
CLUSTERS = 2048
NEAR_CAP = 192
FAR_CAP = 512
NEAR_TOTAL = 24576
FAR_TOTAL = 65536


def near_pairs(key):
    base = jax.random.fold_in(key, 11)
    key_row, key_offset, key_col = jax.random.split(base, 3)
    slot_ids = jnp.arange(NEAR_TOTAL, dtype=jnp.int32)
    group_ids = slot_ids // NEAR_CAP
    within = slot_ids % NEAR_CAP
    row_pick = jax.random.randint(key_row, (NEAR_TOTAL,), 0, CL, dtype=jnp.int32)
    offset = jax.random.randint(key_offset, (NEAR_TOTAL,), -1, 2, dtype=jnp.int32)
    col_pick = jax.random.randint(key_col, (NEAR_TOTAL,), 0, CL, dtype=jnp.int32)
    row_ids = group_ids * CL + jnp.where(within < CL, within, row_pick)
    col_group = jnp.clip(group_ids + offset, 0, GROUPS - 1)
    col_ids = jnp.where(within < CL, row_ids, col_group * CL + col_pick)
    return (row_ids, col_ids)


def draw_near_rows(key, part):
    row_ids, col_ids = near_pairs(key)
    return row_ids


def draw_near_cols(key, part):
    row_ids, col_ids = near_pairs(key)
    return col_ids


def draw_near_count(key, part):
    key = jax.random.fold_in(key, 21)
    key_load, key_full = jax.random.split(key, 2)
    picks = jax.random.randint(key_load, (GROUPS,), NEAR_CAP // 3, NEAR_CAP + 1, dtype=jnp.int32)
    counts = jnp.maximum(picks * picks // NEAR_CAP, CL)
    busiest = jax.random.randint(key_full, (), 0, GROUPS, dtype=jnp.int32)
    counts = jnp.where(jnp.arange(GROUPS, dtype=jnp.int32) == busiest, NEAR_CAP, counts)
    return counts.astype(jnp.int32)


def draw_far_rows(key, part):
    key = jax.random.fold_in(key, 31)
    slot_ids = jnp.arange(FAR_TOTAL, dtype=jnp.int32)
    picks = jax.random.randint(key, (FAR_TOTAL,), 0, CL, dtype=jnp.int32)
    return slot_ids // FAR_CAP * CL + picks


def draw_far_cols(key, part):
    key = jax.random.fold_in(key, 61)
    key_offset, key_jitter, key_pick = jax.random.split(key, 3)
    slot_ids = jnp.arange(FAR_TOTAL, dtype=jnp.int32)
    group_ids = slot_ids // FAR_CAP
    within = slot_ids % FAR_CAP
    residue = within % GROUPS
    offsets = jax.random.randint(key_offset, (GROUPS,), 0, GROUPS, dtype=jnp.int32)
    jitter = jax.random.randint(key_jitter, (FAR_TOTAL,), 0, 2, dtype=jnp.int32)
    jitter = jnp.where(residue == 0, 1, jnp.where(residue == 1, 0, jitter))
    owner = (offsets[group_ids] + residue + jitter) % GROUPS
    picks = jax.random.randint(key_pick, (FAR_TOTAL,), 0, CL, dtype=jnp.int32)
    return (owner * CL + picks).astype(jnp.int32)


def draw_far_rank(key, part):
    key = jax.random.fold_in(key, 41)
    slot_ids = jnp.arange(FAR_TOTAL, dtype=jnp.int32)
    picks = jax.random.randint(key, (FAR_TOTAL,), 4, R + 1, dtype=jnp.int32)
    return jnp.where(slot_ids % FAR_CAP == 0, R, picks).astype(jnp.int32)


def draw_right_side(key, part):
    key = jax.random.fold_in(key, 51)
    key_value = jax.random.fold_in(key, 0)
    cluster = jnp.arange(CLUSTERS, dtype=jnp.float32)[:, None]
    rising = jnp.exp(math.log(3.0) * cluster / max(CLUSTERS - 1, 1))
    values = jnp.clip(jax.random.normal(key_value, (CLUSTERS, M), jnp.float32), -6.0, 6.0)
    result = values * rising
    return result.astype(jnp.float32)


def steps_of(stream_key, shape, cuts, least, largest):
    def one(dim, blocks):
        steps = jax.random.uniform(jax.random.fold_in(jax.random.fold_in(stream_key, 6), dim), (blocks,), jnp.float32, least / len(cuts), largest / len(cuts))
        return jnp.repeat(jnp.exp(steps), shape[dim] // blocks).reshape((-1,) + (1,) * (len(shape) - dim - 1))

    level = one(*cuts[0])
    for cut in cuts[1:]:
        level = level * one(*cut)
    return level


def noise(rng, dims, deviation, limit, cuts=(), kind=jnp.bfloat16):
    factor_of = steps_of(rng, dims, cuts, -0.22, 0.18) if cuts else 1.0
    array = jax.random.normal(rng, dims, jnp.float32) * deviation * factor_of
    return jnp.minimum(jnp.maximum(array, -limit), limit).astype(kind)


def setup_inputs(seed: int = 0) -> dict:
    keys = jax.random.split(jax.random.key(seed), 12)
    return {
        "right_side": draw_right_side(jax.random.fold_in(keys[11], 71), 0),
        "diagonal": jnp.clip(jnp.exp(math.log(2.0) - 1.3862944 * jax.random.uniform(keys[1], (CLUSTERS, M), jnp.float32) ** steps_of(keys[1], (CLUSTERS, M), ((0, 128),), -0.2, 0.2)), 0.5, 2.0),
        "near_blocks": noise(keys[2], (NEAR_TOTAL, M, M), (M * 2 * NEAR_PER) ** -0.5, 0.109375, ((0, 128),)),
        "near_rows": draw_near_rows(jax.random.fold_in(keys[11], 71), 0),
        "near_cols": draw_near_cols(jax.random.fold_in(keys[11], 71), 0),
        "near_count": draw_near_count(jax.random.fold_in(keys[11], 71), 0),
        "basis": noise(keys[6], (CLUSTERS, R, M), M ** -0.5, 0.5, ((0, 128),)),
        "coupling": noise(keys[7], (FAR_TOTAL, R * R), 0.07, 0.41992188, ((0, 128),)),
        "far_rows": draw_far_rows(jax.random.fold_in(keys[11], 71), 0),
        "far_cols": draw_far_cols(jax.random.fold_in(keys[11], 71), 0),
        "far_rank": draw_far_rank(jax.random.fold_in(keys[11], 71), 0),
    }


epsilon = 1e-6


def operate(field, diagonal, blocks, near_row_ids, near_col_ids, near_count, basis_wide, coupled, far_row_ids, far_col_ids):
    field_low = field.astype(jnp.bfloat16)
    field_low = lax.optimization_barrier(field_low)
    field_wide = field_low.astype(jnp.float32)

    def near_step(total, pieces):
        block, row_ids, col_ids, live_count = pieces
        live_slot = (jnp.arange(NEAR_CAP) < live_count).astype(jnp.float32)[:, None]
        block_wide = block.astype(jnp.float32)
        forward = jnp.einsum("kab,kb->ka", block_wide, field_wide[col_ids], precision=lax.Precision.HIGHEST) * live_slot
        backward = jnp.einsum("kab,ka->kb", block_wide, field_wide[row_ids], precision=lax.Precision.HIGHEST) * live_slot
        total = total.at[row_ids].add(forward).at[col_ids].add(backward)
        return total, None

    near_part, _ = lax.scan(near_step, jnp.zeros((CLUSTERS, M), jnp.float32), (blocks, near_row_ids, near_col_ids, near_count))
    coeffs = jnp.einsum("crm,cm->cr", basis_wide, field_wide, precision=lax.Precision.HIGHEST)

    def far_step(total, pieces):
        matrices, row_ids, col_ids = pieces
        forward = jnp.einsum("kab,kb->ka", matrices, coeffs[col_ids], precision=lax.Precision.HIGHEST)
        backward = jnp.einsum("kab,ka->kb", matrices, coeffs[row_ids], precision=lax.Precision.HIGHEST)
        total = total.at[row_ids].add(forward).at[col_ids].add(backward)
        return total, None

    far_sum, _ = lax.scan(far_step, jnp.zeros((CLUSTERS, R), jnp.float32), (coupled, far_row_ids, far_col_ids))
    far_low = far_sum.astype(jnp.bfloat16)
    far_low = lax.optimization_barrier(far_low)
    far_part = jnp.einsum("crm,cr->cm", basis_wide, far_low.astype(jnp.float32), precision=lax.Precision.HIGHEST)
    return diagonal * field + near_part + far_part


def reference(right_side, diagonal, near_blocks, near_rows, near_cols, near_count, basis, coupling, far_rows, far_cols, far_rank):
    blocks = near_blocks.reshape(GROUPS, NEAR_CAP, M, M)
    near_row_ids = near_rows.reshape(GROUPS, NEAR_CAP).astype(jnp.int32)
    near_col_ids = near_cols.reshape(GROUPS, NEAR_CAP).astype(jnp.int32)
    basis_wide = basis.astype(jnp.float32)
    levels = jnp.arange(R, dtype=jnp.int32)
    rank_mask = (levels[None, :, None] < far_rank[:, None, None]) & (levels[None, None, :] < far_rank[:, None, None])
    coupled = jnp.where(rank_mask, coupling.reshape(FAR_TOTAL, R, R).astype(jnp.float32), jnp.float32(0.0))
    coupled = coupled.reshape(GROUPS, FAR_CAP, R, R)
    far_row_ids = far_rows.reshape(GROUPS, FAR_CAP).astype(jnp.int32)
    far_col_ids = far_cols.reshape(GROUPS, FAR_CAP).astype(jnp.int32)
    solution = jnp.zeros_like(right_side)
    residual = right_side
    for sweep in range(ITERS):
        image = operate(residual, diagonal, blocks, near_row_ids, near_col_ids, near_count, basis_wide, coupled, far_row_ids, far_col_ids)
        cross_term = jnp.sum(residual * image)
        square_term = jnp.sum(image * image)
        step_size = cross_term / (square_term + epsilon)
        solution = solution + step_size * residual
        residual = residual - step_size * image
    return solution, residual
```

```python
import functools

import jax
import jax.numpy as jnp
from jax import lax
from jax.experimental import pallas as pl
from jax.experimental.pallas import tpu as pltpu
from jax.sharding import PartitionSpec as P

ITERS = 3
AXES = ("gx", "gy", "gz")
N = 128
CL = 16
M = 128
R = 32
NEAR = 192
FAR = 512
ROWS = 8
EPS = 1e-6
F32, BF16 = jnp.float32, jnp.bfloat16
LOGICAL = pl.DeviceIdType.LOGICAL


def iota(shape, dim):
    return lax.broadcasted_iota(jnp.int32, shape, dim)


def ones_where(cond):
    return jnp.where(cond, 1.0, 0.0).astype(BF16)


def dot(a, b):
    return jnp.dot(a, b, preferred_element_type=F32)


def dot_t(a, b):
    return lax.dot_general(a, b, (((1,), (1,)), ((), ())), preferred_element_type=F32)


def split(x):
    hi = x.astype(BF16)
    return hi, (x - hi.astype(F32)).astype(BF16)


def kernel(
    rs_ref, diag_ref, near_hbm, nrow_ref, ncol_ref, ncount_ref, basis_ref, coup_hbm, frow_ref, fcol_ref, frank_ref,
    sol_ref, res_ref,
    near, coup, big, t8, e2, fold, hrow, hrow_t, gmask, jmask, hnr, hnc, hnr_t, hnc_t, meta,
    gath, grow, backs, fwds, c4s, send, recv, win, spout, spin, last_out, last_in,
    dma_sem, ssem, rsem, wsem_s, wsem_r, psem_s, psem_r, lsem_s, lsem_r,
):
    me = lax.axis_index(AXES)
    nxt, prv = lax.rem(me + 1, N), lax.rem(me + N - 1, N)
    load_coup = pltpu.make_async_copy(coup_hbm, coup, dma_sem.at[0])
    load_near = pltpu.make_async_copy(near_hbm, near, dma_sem.at[1])
    load_coup.start()
    load_near.start()

    barrier = pltpu.get_barrier_semaphore()

    def greet(o, carry):
        pl.semaphore_signal(barrier, inc=1, device_id=lax.rem(me + o, N), device_id_type=LOGICAL)
        return carry

    lax.fori_loop(1, N, greet, 0)

    frow = frow_ref[...] - me * CL
    fcol = fcol_ref[...]
    owner = fcol // CL
    local = fcol - owner * CL
    rank = frank_ref[...]
    owner_f = owner.astype(F32)
    codes = jnp.concatenate(
        [frow.astype(F32), owner_f, local.astype(F32), rank.astype(F32), jnp.zeros((4, FAR), F32)], axis=0
    )
    codes_t = jnp.transpose(codes)
    frow_c = codes_t[:, 0:1].astype(jnp.int32)
    owner_c = codes_t[:, 1:2].astype(jnp.int32)
    local_c = codes_t[:, 2:3].astype(jnp.int32)
    rank_c = codes_t[:, 3:4].astype(jnp.int32)
    same = jnp.where((owner_c == owner) & (iota((FAR, FAR), 0) < iota((FAR, FAR), 1)), 1.0, 0.0)
    place_f = jnp.sum(same, axis=0, keepdims=True)
    place = place_f.astype(jnp.int32)
    place_c = jnp.transpose(jnp.broadcast_to(place_f, (8, FAR)))[:, 0:1].astype(jnp.int32)

    lane = iota((1, M), 1)
    gmask[...] = ones_where(lane // R == local_c % 4)
    jmask[...] = jnp.where(lane // R == place_c % 4, 1.0, 0.0)
    hrow[...] = ones_where(iota((1, CL), 1) == frow_c)
    hrow_t[...] = ones_where(iota((CL, 1), 0) == frow)
    code_g = owner_c * ROWS + local_c // 4
    big[pl.ds(0, FAR), :] = ones_where(iota((1, N * ROWS), 1) == code_g)
    code_s = owner * ROWS + 4 + place // 4
    t8[...] = ones_where(iota((N * ROWS, 1), 0) == code_s)
    e2[...] = ones_where(iota((M, R * R), 0) % R == iota((M, R * R), 1) // R)
    fold[...] = ones_where(iota((2 * M, M), 0) % R == iota((2 * M, M), 1) % R)
    code_m = owner * ROWS + 7
    t7 = ones_where(iota((N * ROWS, 1), 0) == code_m)
    meta[...] = dot(t7, jnp.where(lane == place_c, local_c.astype(F32), 0.0).astype(BF16))
    big[pl.ds(FAR + 64, 16), :] = ones_where(
        (iota((16, N * ROWS), 0) == 0) & (iota((16, N * ROWS), 1) % ROWS == 6)
    )
    count = ncount_ref[0, 0]
    live = iota((1, NEAR), 1) < count
    nrow = nrow_ref[...] - me * CL
    ncol = ncol_ref[...] - me * CL + CL
    hnr_t[...] = ones_where((iota((CL, 1), 0) == nrow) & live)
    hnc_t[...] = ones_where((iota((3 * CL, 1), 0) == ncol) & live)
    ncodes = jnp.concatenate([nrow.astype(F32), ncol.astype(F32), jnp.zeros((6, NEAR), F32)], axis=0)
    ncodes_t = jnp.transpose(ncodes)
    hnr[...] = ones_where(iota((1, CL), 1) == ncodes_t[:, 0:1].astype(jnp.int32))
    hnc[...] = ones_where(iota((1, 3 * CL), 1) == ncodes_t[:, 1:2].astype(jnp.int32))

    load_coup.wait()
    ab = iota((1, R * R), 1)
    top = jnp.maximum(ab // R, ab % R)
    coup[...] = jnp.where(top < rank_c, coup[...].astype(F32), 0.0).astype(BF16)

    own = iota((CL, CL * R), 1) // R == iota((CL, CL * R), 0)
    rows_of = ones_where(iota((ROWS, CL), 1) // 4 == iota((ROWS, CL), 0))
    even = iota((NEAR, 1), 0) % 2 == 0
    pair_of_row = iota((16, 1), 0) // 2
    odd_row = iota((16, 1), 0) % 2 == 1

    field = rs_ref[...]
    residual = field
    solution = jnp.zeros_like(field)
    sums_tile = jnp.zeros((ROWS, M), F32)
    sub8 = iota((ROWS, M), 0)
    lane8 = iota((ROWS, M), 1)
    image = field

    def to_rows(rw, ww):
        tile = jnp.zeros((ROWS, M), F32)
        for i, value in enumerate((rw, ww)):
            rest = jnp.full((ROWS, M), value, F32)
            for part in range(3):
                piece = rest.astype(BF16).astype(F32)
                rest = rest - piece
                tile = tile + jnp.where((sub8 == 6) & (lane8 == 3 * i + part), piece, 0.0)
        return tile

    for t in range(ITERS):
        low = field.astype(BF16)
        win[t, 1] = low
        if t == 0:
            pl.semaphore_wait(barrier, N - 1)
        to_next = pltpu.make_async_remote_copy(
            win.at[t, 1], win.at[t, 0], wsem_s.at[t, 0], wsem_r.at[t, 0], device_id=nxt, device_id_type=LOGICAL
        )
        to_prev = pltpu.make_async_remote_copy(
            win.at[t, 1], win.at[t, 2], wsem_s.at[t, 1], wsem_r.at[t, 1], device_id=prv, device_id_type=LOGICAL
        )
        to_next.start()
        to_prev.start()

        raw = jnp.where(own, dot_t(low, basis_ref[...]), 0.0)
        coeffs = (raw[:, 0:M] + raw[:, M : 2 * M] + raw[:, 2 * M : 3 * M] + raw[:, 3 * M : 4 * M]).astype(BF16)
        cexp = dot(coeffs, e2[...]).astype(BF16)
        for i in range(8):
            part = pl.ds(i * 64, 64)
            wide = dot(hrow[part, :], cexp)
            prod = coup[part, :].astype(F32) * wide
            acc = prod[:, 0:M]
            for j in range(1, 8):
                acc = acc + prod[:, j * M : (j + 1) * M]
            hi, lo = split(acc)
            summed = dot(jnp.concatenate([hi, lo], axis=1), fold[...])
            c4s[part, :] = (summed * jmask[part, :]).astype(BF16)
        tile = dot(rows_of, coeffs) + sums_tile
        message = dot(t8[...], c4s[...])
        if t == 0:
            message = message + meta[...]
        send[t] = (message.reshape(N, ROWS, M) + tile[None]).astype(BF16)
        recv[t, me] = send[t, me]

        grow_t = dot(hnr[...], low)
        zero = jnp.zeros_like(grow_t)
        grow[...] = jnp.concatenate([jnp.where(even, grow_t, zero), jnp.where(even, zero, grow_t)], axis=1).astype(BF16)

        def far_copy(o, t=t):
            there = lax.rem(me + o, N)
            return pltpu.make_async_remote_copy(
                send.at[t, there], recv.at[t, me], ssem.at[t], rsem.at[t], device_id=there, device_id_type=LOGICAL
            )

        if t == 0:
            load_near.wait()

        for o in range(1, 8):
            far_copy(o).start()

        def near_back(i, carry, far_copy=far_copy):
            for u in range(10):
                far_copy(8 + i * 10 + u).start()
            part = pl.ds(pl.multiple_of(i * 16, 16), 16)
            lhs = grow[part, :]
            out = jnp.zeros((16, M), F32)
            for j in range(8):
                block = near[pl.ds(pl.multiple_of(i * 16 + 2 * j, 2), 2)].reshape(2 * M, M)
                out = jnp.where(pair_of_row == j, dot(lhs, block), out)
            backs[part, :] = out
            return carry

        lax.fori_loop(0, 12, near_back, 0)
        hi, lo = split(backs[...])
        spilled = dot(hnc_t[...], hi) + dot(hnc_t[...], lo)
        spout[t, 0] = spilled[0:CL]
        spout[t, 1] = spilled[2 * CL : 3 * CL]
        spill_prev = pltpu.make_async_remote_copy(
            spout.at[t, 0], spin.at[t, 1], psem_s.at[t, 0], psem_r.at[t, 1], device_id=prv, device_id_type=LOGICAL
        )
        spill_next = pltpu.make_async_remote_copy(
            spout.at[t, 1], spin.at[t, 0], psem_s.at[t, 1], psem_r.at[t, 0], device_id=nxt, device_id_type=LOGICAL
        )
        spill_prev.start()
        spill_next.start()

        to_next.wait_recv()
        to_prev.wait_recv()
        gath[...] = dot(hnc[...], win[t].reshape(3 * CL, M)).astype(BF16)

        def near_forward(i, carry):
            part = pl.ds(pl.multiple_of(i * 16, 16), 16)
            lhs = gath[part, :]
            out = jnp.zeros((16, M), F32)
            for j in range(8):
                block = near[pl.ds(pl.multiple_of(i * 16 + 2 * j, 2), 2)].reshape(2 * M, M)
                got = dot_t(lhs, block)
                got = jnp.where(odd_row, got[:, M:], got[:, :M])
                out = jnp.where(pair_of_row == j, got, out)
            fwds[part, :] = out
            return carry

        lax.fori_loop(0, 12, near_forward, 0)
        hi, lo = split(fwds[...])
        product = diag_ref[...] * field + spilled[CL : 2 * CL] + dot(hnr_t[...], hi) + dot(hnr_t[...], lo)

        everyone = recv.at[t, pl.ds(0, N - 1)]
        pltpu.make_async_copy(everyone, everyone, rsem.at[t]).wait()
        arrived = recv[t].reshape(N * ROWS, M)
        if t == 0:
            pick = ones_where(iota((16, M), 1) == iota((16, M), 0))
            numbers = dot_t(pick, arrived)
            col = iota((1, N * ROWS), 1) % ROWS
            first = jnp.concatenate([numbers[:, 3:], numbers[:, :3]], axis=1)
            second = jnp.concatenate([numbers[:, 2:], numbers[:, :2]], axis=1)
            pieces = []
            for q in range(4):
                number = jnp.where(col == 4, first[q : q + 1], jnp.where(col == 5, second[4 + q : 5 + q], -1.0))
                pieces.append(ones_where(iota((CL, 1), 0).astype(F32) == number))
            big[pl.ds(FAR, 64), :] = jnp.concatenate(pieces, axis=0)
        got = dot(big[...], arrived)
        totals = got[FAR + 64 : FAR + 65, :]
        c4s[...] = dot(got[0:FAR].astype(BF16) * gmask[...], fold[0:M, :]).astype(BF16)
        z = jnp.zeros((CL, R * R), F32)
        for i in range(4):
            part = pl.ds(i * 128, 128)
            c4 = c4s[part, :].astype(F32)
            prods = coup[part, :].astype(F32) * jnp.concatenate([c4] * 8, axis=1)
            hi, lo = split(prods)
            z = z + dot(hrow_t[:, i * 128 : (i + 1) * 128], hi) + dot(hrow_t[:, i * 128 : (i + 1) * 128], lo)
        hi, lo = split(z)
        farsum = dot_t(hi, e2[...]) + dot_t(lo, e2[...])
        slots = jnp.zeros((CL, M), F32)
        for q in range(4):
            slots = slots + jnp.where(lane // R == q, got[FAR + 16 * q : FAR + 16 * (q + 1), :], 0.0)
        hi, lo = split(slots)
        farsum = farsum + dot(jnp.concatenate([hi, lo], axis=1), fold[...])
        diag_far = jnp.where(own, jnp.concatenate([farsum] * 4, axis=1), 0.0).astype(BF16)
        product = product + dot(diag_far, basis_ref[...])

        spill_prev.wait_recv()
        spill_next.wait_recv()
        product = product + spin[t, 0] + spin[t, 1]

        if t == 0:
            image = product
        else:
            rw = totals[:, 0:1] + totals[:, 1:2] + totals[:, 2:3]
            ww = totals[:, 3:4] + totals[:, 4:5] + totals[:, 5:6]
            step = rw / (ww + EPS)
            solution = solution + step * residual
            residual = residual - step * image
            image = image - step * product
        field = image
        if t + 1 < ITERS:
            sums_tile = to_rows(jnp.sum(residual * image), jnp.sum(image * image))

    rw, ww = jnp.sum(residual * image), jnp.sum(image * image)
    last_out[...] = jnp.where(lane == 0, rw, jnp.where(lane == 1, ww, 0.0))
    last_in[me] = last_out[...]

    def last_copy(o, carry):
        pltpu.make_async_remote_copy(
            last_out, last_in.at[me], lsem_s, lsem_r, device_id=lax.rem(me + o, N), device_id_type=LOGICAL
        ).start()
        return carry

    lax.fori_loop(1, N, last_copy, 0)
    everyone = last_in.at[pl.ds(0, N - 1)]
    pltpu.make_async_copy(everyone, everyone, lsem_r).wait()
    totals = jnp.sum(last_in[...], axis=0)
    step = totals[:, 0:1] / (totals[:, 1:2] + EPS)
    sol_ref[...] = solution + step * residual
    res_ref[...] = residual - step * image

    pltpu.make_async_copy(everyone, everyone, lsem_s).wait()
    for t in range(ITERS):
        sent = send.at[t, pl.ds(0, N - 1)]
        pltpu.make_async_copy(sent, sent, ssem.at[t]).wait()
        for i in range(2):
            pltpu.make_async_copy(win.at[t, 1], win.at[t, 1], wsem_s.at[t, i]).wait()
            pltpu.make_async_copy(spout.at[t, i], spout.at[t, i], psem_s.at[t, i]).wait()


def on_device(rs, diag, near, nrow, ncol, ncount, basis, coup, frow, fcol, frank):
    vmem = pl.BlockSpec(memory_space=pltpu.VMEM)
    smem = pl.BlockSpec(memory_space=pltpu.SMEM)
    hbm = pl.BlockSpec(memory_space=pl.ANY)
    v = pltpu.VMEM
    dma = pltpu.SemaphoreType.DMA
    shape = jax.ShapeDtypeStruct((CL, M), F32)
    return pl.pallas_call(
        kernel,
        out_shape=(shape, shape),
        in_specs=[vmem, vmem, hbm, vmem, vmem, smem, vmem, hbm, vmem, vmem, vmem],
        out_specs=(vmem, vmem),
        scratch_shapes=[
            v((NEAR, M, M), BF16),
            v((FAR, R * R), BF16),
            v((FAR + 80, N * ROWS), BF16),
            v((N * ROWS, FAR), BF16),
            v((M, R * R), BF16),
            v((2 * M, M), BF16),
            v((FAR, CL), BF16),
            v((CL, FAR), BF16),
            v((FAR, M), BF16),
            v((FAR, M), F32),
            v((NEAR, CL), BF16),
            v((NEAR, 3 * CL), BF16),
            v((CL, NEAR), BF16),
            v((3 * CL, NEAR), BF16),
            v((N * ROWS, M), F32),
            v((NEAR, M), BF16),
            v((NEAR, 2 * M), BF16),
            v((NEAR, M), F32),
            v((NEAR, M), F32),
            v((FAR, M), BF16),
            v((ITERS, N, ROWS, M), BF16),
            v((ITERS, N, ROWS, M), BF16),
            v((ITERS, 3, CL, M), BF16),
            v((ITERS, 2, CL, M), F32),
            v((ITERS, 2, CL, M), F32),
            v((1, M), F32),
            v((N, 1, M), F32),
            dma((2,)),
            dma((ITERS,)),
            dma((ITERS,)),
            dma((ITERS, 2)),
            dma((ITERS, 2)),
            dma((ITERS, 2)),
            dma((ITERS, 2)),
            dma,
            dma,
        ],
        compiler_params=pltpu.CompilerParams(
            collective_id=0, has_side_effects=True, vmem_limit_bytes=48 << 20
        ),
    )(
        rs,
        diag,
        near,
        nrow.reshape(1, NEAR),
        ncol.reshape(1, NEAR),
        ncount.reshape(1, 1),
        basis.reshape(CL * R, M),
        coup,
        frow.reshape(1, FAR),
        fcol.reshape(1, FAR),
        frank.reshape(1, FAR),
    )


def solution(mesh):
    flat = P(AXES)
    two = P(AXES, None)
    three = P(AXES, None, None)
    return jax.shard_map(
        on_device,
        mesh=mesh,
        in_specs=(two, two, three, flat, flat, flat, three, two, flat, flat, flat),
        out_specs=(two, two),
        check_vma=False,
    )
```

```python
import functools

import jax
import jax.numpy as jnp
from jax import lax
from jax.experimental import pallas as pl
from jax.experimental.pallas import tpu as pltpu
from jax.sharding import PartitionSpec as P

ITERS = 3
AXES = ("gx", "gy", "gz")
N = 128
CL = 16
M = 128
R = 32
NEAR = 192
FAR = 512
ROWS = 8
EPS = 1e-6
F32, BF16 = jnp.float32, jnp.bfloat16
LOGICAL = pl.DeviceIdType.LOGICAL


STEPS = sorted(
    ((code, core) for code in range(64) for core in range(2) if (code, core) != (0, 0)),
    key=lambda s: (-bin(s[0]).count("1"), s[0], s[1]),
)
GRAY = (0, 1, 3, 2)
FIRST = 44


def partners():
    gx, gy, gz = lax.axis_index("gx"), lax.axis_index("gy"), lax.axis_index("gz")
    x, core = gx // 2, gx % 2
    xs = [((x + step) % 4) * 32 for step in range(4)]
    cores = [core * 16, (1 - core) * 16]
    zs = [((gy + step) % 4) * 4 for step in range(4)]
    ys = [(gz + step) % 4 for step in range(4)]
    return [
        xs[GRAY[code // 16]] + cores[other] + zs[GRAY[code // 4 % 4]] + ys[GRAY[code % 4]] for code, other in STEPS
    ]


def iota(shape, dim):
    return lax.broadcasted_iota(jnp.int32, shape, dim)


def ones_where(cond):
    return jnp.where(cond, 1.0, 0.0).astype(BF16)


def dot(a, b):
    return jnp.dot(a, b, preferred_element_type=F32)


def dot_t(a, b):
    return lax.dot_general(a, b, (((1,), (1,)), ((), ())), preferred_element_type=F32)


def copies(x):
    x = x + pltpu.roll(x, 2 * R, 1)
    return x + pltpu.roll(x, R, 1)


def whole(x):
    return jnp.sum(jnp.sum(x, axis=0, keepdims=True), axis=1, keepdims=True)


def split(x):
    hi = x.astype(BF16)
    return hi, (x - hi.astype(F32)).astype(BF16)


def kernel(
    rs_hbm, diag_hbm, near_hbm, nrow_hbm, ncol_hbm, ncount_hbm, basis_hbm, coup_hbm, frow_hbm, fcol_hbm, frank_hbm,
    out_ref,
    rs_ref, diag_ref, nrow_ref, ncol_ref, ncount_ref, basis_ref, frow_ref, fcol_ref, frank_ref,
    near, coup, coup_t, big, t8, e2_t, basis_t, hrow, hrow_t, gmask, jmask, hnr, hnc, hnr_t, hnc_t, meta,
    gath, grow, backs, fwds, c4s, send, recv, win, spout, spin, last_out, last_in,
    dma_sem, ssem, rsem, wsem_s, wsem_r, psem_s, psem_r, lsem_s, lsem_r,
):
    me = lax.axis_index(AXES)
    nxt, prv = lax.rem(me + 1, N), lax.rem(me + N - 1, N)
    load_coup = pltpu.make_async_copy(coup_hbm, coup, dma_sem.at[0])
    load_near = pltpu.make_async_copy(near_hbm, near, dma_sem.at[1])
    pairs = (
        (frow_hbm, frow_ref), (fcol_hbm, fcol_ref), (frank_hbm, frank_ref), (nrow_hbm, nrow_ref), (ncol_hbm, ncol_ref),
        (ncount_hbm, ncount_ref), (rs_hbm, rs_ref), (basis_hbm, basis_ref), (diag_hbm, diag_ref),
    )
    loads = [pltpu.make_async_copy(a, b, dma_sem.at[2 + i]) for i, (a, b) in enumerate(pairs)]
    for load in loads:
        load.start()
    load_coup.start()
    load_near.start()

    barrier = pltpu.get_barrier_semaphore()

    others = partners()
    for there in others:
        pl.semaphore_signal(barrier, inc=1, device_id=there, device_id_type=LOGICAL)
    for load in loads:
        load.wait()

    frow = frow_ref[...] - me * CL
    fcol = fcol_ref[...]
    owner = fcol // CL
    local = fcol - owner * CL
    rank = frank_ref[...]
    owner_f = owner.astype(F32)
    codes = jnp.concatenate(
        [frow.astype(F32), owner_f, local.astype(F32), rank.astype(F32), jnp.zeros((4, FAR), F32)], axis=0
    )
    codes_t = jnp.transpose(codes)
    frow_c = codes_t[:, 0:1].astype(jnp.int32)
    owner_c = codes_t[:, 1:2].astype(jnp.int32)
    local_c = codes_t[:, 2:3].astype(jnp.int32)
    rank_c = codes_t[:, 3:4].astype(jnp.int32)
    same = jnp.where((owner_c == owner) & (iota((FAR, FAR), 0) < iota((FAR, FAR), 1)), 1.0, 0.0)
    place_f = jnp.sum(same, axis=0, keepdims=True)
    place = place_f.astype(jnp.int32)
    place_c = jnp.transpose(jnp.broadcast_to(place_f, (8, FAR)))[:, 0:1].astype(jnp.int32)

    lane = iota((1, M), 1)
    gmask[...] = jnp.where(lane // R == local_c % 4, 1.0, 0.0)
    jmask[...] = jnp.where(lane // R == place_c % 4, 1.0, 0.0)
    hrow[...] = ones_where(iota((1, CL), 1) == frow_c)
    hrow_t[...] = ones_where(iota((CL, 1), 0) == frow)
    code_g = owner_c * ROWS + local_c // 4
    big[pl.ds(0, FAR), :] = ones_where(iota((1, N * ROWS), 1) == code_g)
    code_s = owner * ROWS + 4 + place // 4
    t8[...] = ones_where(iota((N * ROWS, 1), 0) == code_s)
    e2_t[...] = ones_where(iota((R * R, M), 0) // R == iota((R * R, M), 1) % R)
    eye = ones_where(iota((M, M), 0) == iota((M, M), 1))
    basis_t[...] = dot_t(eye, basis_ref[...]).astype(BF16)
    code_m = owner * ROWS + 7
    t7 = ones_where(iota((N * ROWS, 1), 0) == code_m)
    meta[...] = dot(t7, jnp.where(lane == place_c, local_c.astype(F32), 0.0).astype(BF16))
    big[pl.ds(FAR + 64, 16), :] = ones_where(
        (iota((16, N * ROWS), 0) == 0) & (iota((16, N * ROWS), 1) % ROWS == 6)
    )
    count = ncount_ref[0, 0]
    live = iota((1, NEAR), 1) < count
    nrow = nrow_ref[...] - me * CL
    ncol = ncol_ref[...] - me * CL + CL
    hnr_t[...] = ones_where((iota((CL, 1), 0) == nrow) & live)
    hnc_t[...] = ones_where((iota((3 * CL, 1), 0) == ncol) & live)
    ncodes = jnp.concatenate([nrow.astype(F32), ncol.astype(F32), jnp.zeros((6, NEAR), F32)], axis=0)
    ncodes_t = jnp.transpose(ncodes)
    hnr[...] = ones_where(iota((1, CL), 1) == ncodes_t[:, 0:1].astype(jnp.int32))
    hnc[...] = ones_where(iota((1, 3 * CL), 1) == ncodes_t[:, 1:2].astype(jnp.int32))

    load_coup.wait()
    ab = iota((1, R * R), 1)
    top = jnp.maximum(ab // R, ab % R)
    coup[...] = jnp.where(top < rank_c, coup[...].astype(F32), 0.0).astype(BF16)
    flip = ones_where(iota((R * R, 1), 0) == (ab % R) * R + ab // R)
    for i in range(4):
        part = pl.ds(i * 128, 128)
        coup_t[part, :] = dot(coup[part, :], flip).astype(BF16)

    own = iota((CL, CL * R), 1) // R == iota((CL, CL * R), 0)
    rows_of = ones_where(iota((ROWS, CL), 1) // 4 == iota((ROWS, CL), 0))
    even = iota((NEAR, 1), 0) % 2 == 0
    pair_of_row = iota((16, 1), 0) // 2
    odd_row = iota((16, 1), 0) % 2 == 1

    field = rs_ref[...]
    residual = field
    solution = jnp.zeros_like(field)
    sums_tile = jnp.zeros((ROWS, M), F32)
    sub8 = iota((ROWS, M), 0)
    lane8 = iota((ROWS, M), 1)
    image = field

    def to_rows(rw, ww):
        tile = jnp.zeros((ROWS, M), F32)
        for i, value in enumerate((rw, ww)):
            rest = jnp.broadcast_to(value, (ROWS, M))
            for part in range(3):
                piece = rest.astype(BF16).astype(F32)
                rest = rest - piece
                tile = tile + jnp.where((sub8 == 6) & (lane8 == 3 * i + part), piece, 0.0)
        return tile

    for t in range(ITERS):
        low = field.astype(BF16)
        win[t, 1] = low
        if t == 0:
            pl.semaphore_wait(barrier, N - 1)
        to_next = pltpu.make_async_remote_copy(
            win.at[t, 1], win.at[t, 0], wsem_s.at[t, 0], wsem_r.at[t, 0], device_id=nxt, device_id_type=LOGICAL
        )
        to_prev = pltpu.make_async_remote_copy(
            win.at[t, 1], win.at[t, 2], wsem_s.at[t, 1], wsem_r.at[t, 1], device_id=prv, device_id_type=LOGICAL
        )
        to_next.start()
        to_prev.start()

        raw = jnp.where(own, dot(low, basis_t[...]), 0.0)
        coeffs = (raw[:, 0:M] + raw[:, M : 2 * M] + raw[:, 2 * M : 3 * M] + raw[:, 3 * M : 4 * M]).astype(BF16)
        wide = dot(hrow[...], copies(coeffs.astype(F32)).astype(BF16)).astype(BF16)
        if t == 0:
            for i in range(4):
                part = pl.ds(i * 128, 128)
                prods = coup_t[part, :].astype(F32) * jnp.concatenate([wide[i * 128 : (i + 1) * 128].astype(F32)] * 8, axis=1)
                hi, lo = split(prods)
                c4s[part, :] = ((dot(hi, e2_t[...]) + dot(lo, e2_t[...])) * jmask[part, :]).astype(BF16)
        else:
            prods = coup_t[...] * jnp.concatenate([wide] * 8, axis=1)
            c4s[...] = (dot(prods, e2_t[...]) * jmask[...]).astype(BF16)
        tile = dot(rows_of, coeffs) + sums_tile
        message = dot(t8[...], c4s[...])
        if t == 0:
            message = message + meta[...]
        send[t] = (message.reshape(N, ROWS, M) + tile[None]).astype(BF16)
        recv[t, me] = send[t, me]

        grow_t = dot(hnr[...], low)
        zero = jnp.zeros_like(grow_t)
        grow[...] = jnp.concatenate([jnp.where(even, grow_t, zero), jnp.where(even, zero, grow_t)], axis=1).astype(BF16)

        def far_copy(there, t=t):
            return pltpu.make_async_remote_copy(
                send.at[t, there], recv.at[t, me], ssem.at[t], rsem.at[t], device_id=there, device_id_type=LOGICAL
            )

        for there in others[:FIRST]:
            far_copy(there).start()

        if t == 0:
            load_near.wait()

        def near_back(i, carry):
            for there in others[FIRST + 7 * i : FIRST + 7 * i + 7]:
                far_copy(there).start()
            part = pl.ds(i * 16, 16)
            lhs = grow[part, :]
            out = jnp.zeros((16, M), F32)
            for j in range(8):
                block = near[pl.ds(i * 16 + 2 * j, 2)].reshape(2 * M, M)
                out = jnp.where(pair_of_row == j, dot(lhs, block), out)
            backs[part, :] = out
            return carry

        for i in range(12):
            near_back(i, 0)
        hi, lo = split(backs[...])
        spilled = dot(hnc_t[...], hi) + dot(hnc_t[...], lo)
        spout[t, 0] = spilled[0:CL]
        spout[t, 1] = spilled[2 * CL : 3 * CL]
        spill_prev = pltpu.make_async_remote_copy(
            spout.at[t, 0], spin.at[t, 1], psem_s.at[t, 0], psem_r.at[t, 1], device_id=prv, device_id_type=LOGICAL
        )
        spill_next = pltpu.make_async_remote_copy(
            spout.at[t, 1], spin.at[t, 0], psem_s.at[t, 1], psem_r.at[t, 0], device_id=nxt, device_id_type=LOGICAL
        )
        spill_prev.start()
        spill_next.start()

        to_next.wait_recv()
        to_prev.wait_recv()
        gath[...] = dot(hnc[...], win[t].reshape(3 * CL, M)).astype(BF16)

        def near_forward(i, carry):
            part = pl.ds(pl.multiple_of(i * 16, 16), 16)
            lhs = gath[part, :]
            out = jnp.zeros((16, M), F32)
            for j in range(8):
                block = near[pl.ds(pl.multiple_of(i * 16 + 2 * j, 2), 2)].reshape(2 * M, M)
                got = dot_t(lhs, block)
                got = jnp.where(odd_row, got[:, M:], got[:, :M])
                out = jnp.where(pair_of_row == j, got, out)
            fwds[part, :] = out
            return carry

        lax.fori_loop(0, 12, near_forward, 0)
        hi, lo = split(fwds[...])
        product = diag_ref[...] * field + spilled[CL : 2 * CL] + dot(hnr_t[...], hi) + dot(hnr_t[...], lo)

        everyone = recv.at[t, pl.ds(0, N - 1)]
        pltpu.make_async_copy(everyone, everyone, rsem.at[t]).wait()
        arrived = recv[t].reshape(N * ROWS, M)
        if t == 0:
            pick = ones_where(iota((16, M), 1) == iota((16, M), 0))
            numbers = dot_t(pick, arrived)
            col = iota((1, N * ROWS), 1) % ROWS
            first = jnp.concatenate([numbers[:, 3:], numbers[:, :3]], axis=1)
            second = jnp.concatenate([numbers[:, 2:], numbers[:, :2]], axis=1)
            pieces = []
            for q in range(4):
                number = jnp.where(col == 4, first[q : q + 1], jnp.where(col == 5, second[4 + q : 5 + q], -1.0))
                pieces.append(ones_where(iota((CL, 1), 0).astype(F32) == number))
            big[pl.ds(FAR, 64), :] = jnp.concatenate(pieces, axis=0)
        got = dot(big[...], arrived)
        totals = got[FAR + 64 : FAR + 65, :]
        c4s[...] = copies(got[0:FAR] * gmask[...]).astype(BF16)
        if t == 0:
            z = jnp.zeros((CL, R * R), F32)
            for i in range(4):
                part = pl.ds(i * 128, 128)
                c4 = c4s[part, :].astype(F32)
                hi, lo = split(coup[part, :].astype(F32) * jnp.concatenate([c4] * 8, axis=1))
                rows = hrow_t[:, i * 128 : (i + 1) * 128]
                z = z + dot(rows, hi) + dot(rows, lo)
        else:
            z = dot(hrow_t[...], coup[...] * jnp.concatenate([c4s[...]] * 8, axis=1))
        hi, lo = split(z)
        farsum = dot(jnp.concatenate([hi, lo], axis=0), e2_t[...])
        farsum = farsum[0:CL] + farsum[CL:]
        slots = jnp.zeros((CL, M), F32)
        for q in range(4):
            slots = slots + jnp.where(lane // R == q, got[FAR + 16 * q : FAR + 16 * (q + 1), :], 0.0)
        farsum = farsum + copies(slots)
        diag_far = jnp.where(own, jnp.concatenate([farsum] * 4, axis=1), 0.0).astype(BF16)
        product = product + dot(diag_far, basis_ref[...])

        spill_prev.wait_recv()
        spill_next.wait_recv()
        product = product + spin[t, 0] + spin[t, 1]

        if t == 0:
            image = product
        else:
            rw = totals[:, 0:1] + totals[:, 1:2] + totals[:, 2:3]
            ww = totals[:, 3:4] + totals[:, 4:5] + totals[:, 5:6]
            step = rw / (ww + EPS)
            solution = solution + step * residual
            residual = residual - step * image
            image = image - step * product
        field = image
        if t + 1 < ITERS:
            sums_tile = to_rows(whole(residual * image), whole(image * image))

    rw, ww = whole(residual * image), whole(image * image)
    last_out[...] = jnp.where(lane == 0, rw, jnp.where(lane == 1, ww, 0.0))
    last_in[me] = last_out[...]

    for there in others:
        pltpu.make_async_remote_copy(
            last_out, last_in.at[me], lsem_s, lsem_r, device_id=there, device_id_type=LOGICAL
        ).start()
    everyone = last_in.at[pl.ds(0, N - 1)]
    pltpu.make_async_copy(everyone, everyone, lsem_r).wait()
    totals = jnp.sum(last_in[...], axis=0)
    step = totals[:, 0:1] / (totals[:, 1:2] + EPS)
    out_ref[0] = solution
    out_ref[1] = residual
    out_ref[2] = image
    out_ref[3] = jnp.broadcast_to(step, (CL, M))

    pltpu.make_async_copy(everyone, everyone, lsem_s).wait()
    for t in range(ITERS):
        sent = send.at[t, pl.ds(0, N - 1)]
        pltpu.make_async_copy(sent, sent, ssem.at[t]).wait()
        for i in range(2):
            pltpu.make_async_copy(win.at[t, 1], win.at[t, 1], wsem_s.at[t, i]).wait()
            pltpu.make_async_copy(spout.at[t, i], spout.at[t, i], psem_s.at[t, i]).wait()


def on_device(rs, diag, near, nrow, ncol, ncount, basis, coup, frow, fcol, frank):
    vmem = pl.BlockSpec(memory_space=pltpu.VMEM)
    hbm = pl.BlockSpec(memory_space=pl.ANY)
    ints = jnp.int32
    v = pltpu.VMEM
    dma = pltpu.SemaphoreType.DMA
    out = pl.pallas_call(
        kernel,
        out_shape=jax.ShapeDtypeStruct((4, CL, M), F32),
        in_specs=[hbm] * 11,
        out_specs=vmem,
        scratch_shapes=[
            v((CL, M), F32),
            v((CL, M), F32),
            v((1, NEAR), ints),
            v((1, NEAR), ints),
            pltpu.SMEM((1, 1), ints),
            v((CL * R, M), BF16),
            v((1, FAR), ints),
            v((1, FAR), ints),
            v((1, FAR), ints),
            v((NEAR, M, M), BF16),
            v((FAR, R * R), BF16),
            v((FAR, R * R), BF16),
            v((FAR + 80, N * ROWS), BF16),
            v((N * ROWS, FAR), BF16),
            v((R * R, M), BF16),
            v((M, CL * R), BF16),
            v((FAR, CL), BF16),
            v((CL, FAR), BF16),
            v((FAR, M), F32),
            v((FAR, M), F32),
            v((NEAR, CL), BF16),
            v((NEAR, 3 * CL), BF16),
            v((CL, NEAR), BF16),
            v((3 * CL, NEAR), BF16),
            v((N * ROWS, M), F32),
            v((NEAR, M), BF16),
            v((NEAR, 2 * M), BF16),
            v((NEAR, M), F32),
            v((NEAR, M), F32),
            v((FAR, M), BF16),
            v((ITERS, N, ROWS, M), BF16),
            v((ITERS, N, ROWS, M), BF16),
            v((ITERS, 3, CL, M), BF16),
            v((ITERS, 2, CL, M), F32),
            v((ITERS, 2, CL, M), F32),
            v((1, M), F32),
            v((N, 1, M), F32),
            dma((11,)),
            dma((ITERS,)),
            dma((ITERS,)),
            dma((ITERS, 2)),
            dma((ITERS, 2)),
            dma((ITERS, 2)),
            dma((ITERS, 2)),
            dma,
            dma,
        ],
        compiler_params=pltpu.CompilerParams(
            collective_id=0, has_side_effects=True, vmem_limit_bytes=60 << 20
        ),
    )(
        rs,
        diag,
        near,
        nrow.reshape(1, NEAR),
        ncol.reshape(1, NEAR),
        ncount.reshape(1, 1),
        basis.reshape(CL * R, M),
        coup,
        frow.reshape(1, FAR),
        fcol.reshape(1, FAR),
        frank.reshape(1, FAR),
    )
    return out[0] + out[3] * out[1], out[1] - out[3] * out[2]


def solution(mesh):
    flat = P(AXES)
    two = P(AXES, None)
    three = P(AXES, None, None)
    return jax.shard_map(
        on_device,
        mesh=mesh,
        in_specs=(two, two, three, flat, flat, flat, three, two, flat, flat, flat),
        out_specs=(two, two),
        check_vma=False,
    )
```

```python
import functools

import jax
import jax.numpy as jnp
import numpy as np
from jax import lax
from jax.experimental import pallas as pl
from jax.experimental.pallas import tpu as pltpu
from jax.sharding import PartitionSpec as P

ITERS = 3
AXES = ("gx", "gy", "gz")
N = 128
CL = 16
M = 128
R = 32
NEAR = 192
FAR = 512
ROWS = 8
EPS = 1e-6
F32, BF16 = jnp.float32, jnp.bfloat16
LOGICAL = pl.DeviceIdType.LOGICAL


STEPS = sorted(
    ((code, core) for code in range(64) for core in range(2) if (code, core) != (0, 0)),
    key=lambda s: (-bin(s[0]).count("1"), s[0], s[1]),
)
GRAY = (0, 1, 3, 2)
SHORT = 2
PLANE = sorted(range(1, 16), key=lambda o: -min(o // 4, 4 - o // 4) - min(o % 4, 4 - o % 4))
FIRST = 48
NEXT = 6
PLACE = {step: i for i, step in enumerate(STEPS)}
BACK = [
    PLACE[(sum((0, 2, 1, 3)[code >> shift & 3] << shift for shift in (0, 2, 4)), core)] for code, core in STEPS
]


def order_table():
    steps = STEPS + [(0, 0)]
    table = np.zeros((8, N * (ROWS + 4)), np.int32)
    for i, (code, core) in enumerate(steps):
        for part in (slice(i * ROWS, (i + 1) * ROWS), slice(N * ROWS + i * 4, N * ROWS + (i + 1) * 4)):
            table[0, part] = GRAY[code // 16]
            table[1, part] = core
            table[2, part] = GRAY[code // 4 % 4]
            table[3, part] = GRAY[code % 4]
    return table


def partners():
    gx, gy, gz = lax.axis_index("gx"), lax.axis_index("gy"), lax.axis_index("gz")
    x, core = gx // 2, gx % 2
    xs = [((x + step) % 4) * 32 for step in range(4)]
    cores = [core * 16, (1 - core) * 16]
    zs = [((gy + step) % 4) * 4 for step in range(4)]
    ys = [(gz + step) % 4 for step in range(4)]
    return [
        xs[GRAY[code // 16]] + cores[other] + zs[GRAY[code // 4 % 4]] + ys[GRAY[code % 4]] for code, other in STEPS
    ]


def iota(shape, dim):
    return lax.broadcasted_iota(jnp.int32, shape, dim)


def ones_where(cond):
    return jnp.where(cond, 1.0, 0.0).astype(BF16)


def dot(a, b):
    return jnp.dot(a, b, preferred_element_type=F32)


def dot_t(a, b):
    return lax.dot_general(a, b, (((1,), (1,)), ((), ())), preferred_element_type=F32)


def copies(x):
    x = x + pltpu.roll(x, 2 * R, 1)
    return x + pltpu.roll(x, R, 1)


def whole(x):
    return jnp.sum(jnp.sum(x, axis=0, keepdims=True), axis=1, keepdims=True)


def split(x):
    hi = x.astype(BF16)
    return hi, (x - hi.astype(F32)).astype(BF16)


def kernel(
    rs_hbm, diag_hbm, near_hbm, nrow_hbm, ncol_hbm, ncount_hbm, basis_hbm, coup_hbm, frow_hbm, fcol_hbm, frank_hbm, table_hbm,
    out_ref,
    rs_ref, diag_ref, nrow_ref, ncol_ref, ncount_ref, basis_ref, frow_ref, fcol_ref, frank_ref, table_ref,
    near, coup, coup_t, big, t8, e2_t, basis_t, hrow, hrow_t, gmask, jmask, hnr, hnc, hnr_t, hnc_t, meta,
    big4, t4, pick4, send4, recv4, sum_out, sum_a, sum_mid, sum_b, tree_s, tree_r, gath, grow, backs, fwds, c4s, send, recv, win, spout, spin, last_out, last_in,
    dma_sem, ssem, rsem, wsem_s, wsem_r, psem_s, psem_r, lsem_s, lsem_r,
):
    me = lax.axis_index(AXES)
    nxt, prv = lax.rem(me + 1, N), lax.rem(me + N - 1, N)
    load_coup = pltpu.make_async_copy(coup_hbm, coup, dma_sem.at[0])
    load_near = pltpu.make_async_copy(near_hbm, near, dma_sem.at[1])
    pairs = (
        (frow_hbm, frow_ref), (fcol_hbm, fcol_ref), (frank_hbm, frank_ref), (nrow_hbm, nrow_ref), (ncol_hbm, ncol_ref),
        (ncount_hbm, ncount_ref), (rs_hbm, rs_ref), (basis_hbm, basis_ref), (diag_hbm, diag_ref), (table_hbm, table_ref),
    )
    loads = [pltpu.make_async_copy(a, b, dma_sem.at[2 + i]) for i, (a, b) in enumerate(pairs)]
    for load in loads:
        load.start()
    load_coup.start()
    load_near.start()

    barrier = pltpu.get_barrier_semaphore()

    others = partners()
    for there in others:
        pl.semaphore_signal(barrier, inc=1, device_id=there, device_id_type=LOGICAL)
    for load in loads:
        load.wait()

    frow = frow_ref[...] - me * CL
    fcol = fcol_ref[...]
    owner = fcol // CL
    local = fcol - owner * CL
    rank = frank_ref[...]
    owner_f = owner.astype(F32)
    codes = jnp.concatenate(
        [frow.astype(F32), owner_f, local.astype(F32), rank.astype(F32), jnp.zeros((4, FAR), F32)], axis=0
    )
    codes_t = jnp.transpose(codes)
    frow_c = codes_t[:, 0:1].astype(jnp.int32)
    owner_c = codes_t[:, 1:2].astype(jnp.int32)
    local_c = codes_t[:, 2:3].astype(jnp.int32)
    rank_c = codes_t[:, 3:4].astype(jnp.int32)
    same = jnp.where((owner_c == owner) & (iota((FAR, FAR), 0) < iota((FAR, FAR), 1)), 1.0, 0.0)
    place_f = jnp.sum(same, axis=0, keepdims=True)
    place = place_f.astype(jnp.int32)
    place_c = jnp.transpose(jnp.broadcast_to(place_f, (8, FAR)))[:, 0:1].astype(jnp.int32)

    lane = iota((1, M), 1)
    gmask[...] = jnp.where(lane // R == local_c % 4, 1.0, 0.0)
    jmask[...] = jnp.where(lane // R == place_c % 4, 1.0, 0.0)
    hrow[...] = ones_where(iota((1, CL), 1) == frow_c)
    hrow_t[...] = ones_where(iota((CL, 1), 0) == frow)
    code_g = owner_c * ROWS + local_c // 4
    gx, gy, gz = lax.axis_index("gx"), lax.axis_index("gy"), lax.axis_index("gz")
    t4[:, 0:N] = ones_where(iota((N * 4, N), 0) // 4 == iota((N * 4, N), 1))
    steps = table_ref[...]
    source = (
        (gx // 2 + steps[0:1]) % 4 * 32 + (gx % 2 + steps[1:2]) % 2 * 16 + (gy + steps[2:3]) % 4 * 4 + (gz + steps[3:4]) % 4
    )
    big[pl.ds(0, FAR), :] = ones_where(source[:, 0 : N * ROWS] * ROWS + iota((1, N * ROWS), 1) % ROWS == code_g)
    code_s = owner * ROWS + 4 + place // 4
    t8[...] = ones_where(iota((N * ROWS, 1), 0) == code_s)
    e2_t[...] = ones_where(iota((R * R, M), 0) // R == iota((R * R, M), 1) % R)
    eye = ones_where(iota((M, M), 0) == iota((M, M), 1))
    basis_t[...] = dot_t(eye, basis_ref[...]).astype(BF16)
    code_m = owner * ROWS + 7
    t7 = ones_where(iota((N * ROWS, 1), 0) == code_m)
    meta[...] = dot(t7, jnp.where(lane == place_c, local_c.astype(F32), 0.0).astype(BF16))
    big[pl.ds(FAR + 64, 16), :] = ones_where(
        (iota((16, N * ROWS), 0) == 0) & (iota((16, N * ROWS), 1) % ROWS == 6)
    )
    count = ncount_ref[0, 0]
    live = iota((1, NEAR), 1) < count
    nrow = nrow_ref[...] - me * CL
    ncol = ncol_ref[...] - me * CL + CL
    hnr_t[...] = ones_where((iota((CL, 1), 0) == nrow) & live)
    hnc_t[...] = ones_where((iota((3 * CL, 1), 0) == ncol) & live)
    ncodes = jnp.concatenate([nrow.astype(F32), ncol.astype(F32), jnp.zeros((6, NEAR), F32)], axis=0)
    ncodes_t = jnp.transpose(ncodes)
    hnr[...] = ones_where(iota((1, CL), 1) == ncodes_t[:, 0:1].astype(jnp.int32))
    hnc[...] = ones_where(iota((1, 3 * CL), 1) == ncodes_t[:, 1:2].astype(jnp.int32))

    load_coup.wait()
    ab = iota((1, R * R), 1)
    top = jnp.maximum(ab // R, ab % R)
    coup[...] = jnp.where(top < rank_c, coup[...].astype(F32), 0.0).astype(BF16)
    flip = ones_where(iota((R * R, 1), 0) == (ab % R) * R + ab // R)
    for i in range(4):
        part = pl.ds(i * 128, 128)
        coup_t[part, :] = dot(coup[part, :], flip).astype(BF16)

    own = iota((CL, CL * R), 1) // R == iota((CL, CL * R), 0)
    rows_of = ones_where(iota((ROWS, CL), 1) // 4 == iota((ROWS, CL), 0))
    even = iota((NEAR, 1), 0) % 2 == 0
    even_pair = iota((NEAR, 1), 0) % 4 < 2

    def four_blocks(k):
        first = near[pl.ds(k, 2)].reshape(2 * M, M)
        second = near[pl.ds(k + 2, 2)].reshape(2 * M, M)
        return jnp.concatenate([first, second], axis=1)

    pair_of_row = iota((16, 1), 0) // 2
    odd_row = iota((16, 1), 0) % 2 == 1

    field = rs_ref[...]
    residual = field
    solution = jnp.zeros_like(field)
    sums_tile = jnp.zeros((ROWS, M), F32)
    sub8 = iota((ROWS, M), 0)
    lane8 = iota((ROWS, M), 1)
    image = field

    def to_rows(rw, ww):
        tile = jnp.zeros((ROWS, M), F32)
        for i, value in enumerate((rw, ww)):
            rest = jnp.broadcast_to(value, (ROWS, M))
            for part in range(3):
                piece = rest.astype(BF16).astype(F32)
                rest = rest - piece
                tile = tile + jnp.where((sub8 == 6) & (lane8 == 3 * i + part), piece, 0.0)
        return tile

    for t in range(ITERS):
        low = field.astype(BF16)
        if t >= SHORT:
            sum_out[t - SHORT] = jnp.where(lane == 0, rw, jnp.where(lane == 1, ww, 0.0))
            sum_a[t - SHORT, 0] = sum_out[t - SHORT]
            for o in PLANE:
                pltpu.make_async_remote_copy(
                    sum_out.at[t - SHORT], sum_a.at[t - SHORT, o], tree_s.at[t - SHORT, 0], tree_r.at[t - SHORT, 0],
                    device_id=gx * 16 + (gy + o // 4) % 4 * 4 + (gz + o % 4) % 4, device_id_type=LOGICAL,
                ).start()
        win[t, 1] = low
        if t == 0:
            pl.semaphore_wait(barrier, N - 1)
        to_next = pltpu.make_async_remote_copy(
            win.at[t, 1], win.at[t, 0], wsem_s.at[t, 0], wsem_r.at[t, 0], device_id=nxt, device_id_type=LOGICAL
        )
        to_prev = pltpu.make_async_remote_copy(
            win.at[t, 1], win.at[t, 2], wsem_s.at[t, 1], wsem_r.at[t, 1], device_id=prv, device_id_type=LOGICAL
        )
        to_next.start()
        to_prev.start()

        raw = jnp.where(own, dot(low, basis_t[...]), 0.0)
        coeffs = (raw[:, 0:M] + raw[:, M : 2 * M] + raw[:, 2 * M : 3 * M] + raw[:, 3 * M : 4 * M]).astype(BF16)
        four = copies(coeffs.astype(F32))
        wide = dot(hrow[...], four.astype(BF16)).astype(BF16)
        if t == 0:
            for i in range(4):
                part = pl.ds(i * 128, 128)
                prods = coup_t[part, :].astype(F32) * jnp.concatenate([wide[i * 128 : (i + 1) * 128].astype(F32)] * 8, axis=1)
                hi, lo = split(prods)
                c4s[part, :] = ((dot(hi, e2_t[...]) + dot(lo, e2_t[...])) * jmask[part, :]).astype(BF16)
        else:
            prods = coup_t[...] * jnp.concatenate([wide] * 8, axis=1)
            c4s[...] = (dot(prods, e2_t[...]) * jmask[...]).astype(BF16)
        if t < SHORT:
            message = dot(t8[...], c4s[...])
            tile = dot(rows_of, coeffs) + sums_tile
            if t == 0:
                message = message + meta[...]
            send[t] = (message.reshape(N, ROWS, M) + tile[None]).astype(BF16)
            recv[t, N - 1] = send[t, me]
        else:
            spread4 = jnp.concatenate([jnp.where(lane // R == q, four, 0.0) for q in range(4)] + [jnp.zeros((64, M), F32)], axis=0)
            message = dot(t4[...], c4s[...]) + dot(pick4[...], spread4.astype(BF16))
            send4[t - SHORT] = message.reshape(N, 4, M).astype(BF16)
            recv4[t - SHORT, N - 1] = send4[t - SHORT, N - 1]

        grow_t = dot(hnr[...], low)
        zero = jnp.zeros_like(grow_t)
        grow[...] = jnp.concatenate([jnp.where(even, grow_t, zero), jnp.where(even, zero, grow_t)], axis=1).astype(BF16)

        def far_send(i, t=t):
            there = others[i]
            if t < SHORT:
                src, dst = send.at[t, there], recv.at[t, BACK[i]]
            else:
                src, dst = send4.at[t - SHORT, i], recv4.at[t - SHORT, BACK[i]]
            pltpu.make_async_remote_copy(
                src, dst, ssem.at[t], rsem.at[t], device_id=there, device_id_type=LOGICAL
            ).start()

        for i in range(N - 1):
            far_send(i)

        if t == 0:
            load_near.wait()

        def near_back(i, carry):
            part = pl.ds(i * 16, 16)
            lhs = grow[part, :]
            out = jnp.zeros((16, M), F32)
            for j in range(4):
                out_j = dot(lhs, four_blocks(i * 16 + 4 * j))
                out = jnp.where(pair_of_row == 2 * j, out_j[:, :M], out)
                out = jnp.where(pair_of_row == 2 * j + 1, out_j[:, M:], out)
            backs[part, :] = out
            return carry

        for i in range(12):
            near_back(i, 0)
        hi, lo = split(backs[...])
        spilled = dot(hnc_t[...], hi) + dot(hnc_t[...], lo)
        spout[t, 0] = spilled[0:CL]
        spout[t, 1] = spilled[2 * CL : 3 * CL]
        spill_prev = pltpu.make_async_remote_copy(
            spout.at[t, 0], spin.at[t, 1], psem_s.at[t, 0], psem_r.at[t, 1], device_id=prv, device_id_type=LOGICAL
        )
        spill_next = pltpu.make_async_remote_copy(
            spout.at[t, 1], spin.at[t, 0], psem_s.at[t, 1], psem_r.at[t, 0], device_id=nxt, device_id_type=LOGICAL
        )
        spill_prev.start()
        spill_next.start()
        if t >= SHORT:
            landed = sum_a.at[t - SHORT, pl.ds(1, 15)]
            pltpu.make_async_copy(landed, landed, tree_r.at[t - SHORT, 0]).wait()
            sum_mid[t - SHORT] = jnp.sum(sum_a[t - SHORT], axis=0)
            sum_b[t - SHORT, 0] = sum_mid[t - SHORT]
            for o in (4, 5, 2, 3, 6, 7, 1):
                pltpu.make_async_remote_copy(
                    sum_mid.at[t - SHORT], sum_b.at[t - SHORT, o], tree_s.at[t - SHORT, 1], tree_r.at[t - SHORT, 1],
                    device_id=(gx + o) % 8 * 16 + gy * 4 + gz, device_id_type=LOGICAL,
                ).start()
        if t == SHORT - 1:
            numbers = dot(t4[:, 0 : N], recv[0].astype(F32)[:, 7, :].astype(BF16))
            row4 = iota((N * 4, 1), 0) % 4
            numbers = jnp.where(row4 % 2 == 0, numbers, pltpu.roll(numbers, M - 4, 1))
            spread = ones_where((iota((M, M), 0) == iota((M, M), 1) // CL) & (iota((M, M), 0) < 4))
            numbers = dot(numbers.astype(BF16), spread)
            hot = jnp.where((iota((1, M), 1) % CL).astype(F32) == numbers, 1.0, 0.0)
            hot = jnp.where(iota((1, M), 1) < 64, hot, 0.0)
            pick4[...] = jnp.where(row4 < 2, hot, 0.0).astype(BF16)
            big4[pl.ds(FAR, 64), :] = jnp.transpose(jnp.where(row4 >= 2, hot, 0.0))[0:64, :].astype(BF16)
            source4 = source[:, N * ROWS :]
            col4 = iota((1, N * 4), 1) % 4
            big4[pl.ds(0, FAR), :] = ones_where(source4 * 4 + col4 == owner_c * 4 + place_c // 4)
            source4_c = jnp.transpose(jnp.broadcast_to(source4.astype(F32), (8, N * 4)))[:, 0:1].astype(jnp.int32)
            t4[...] = ones_where(source4_c * 4 + row4 == owner * 4 + 2 + place // 4)

        to_next.wait_recv()
        to_prev.wait_recv()
        gath_t = dot(hnc[...], win[t].reshape(3 * CL, M))
        gath[...] = jnp.concatenate(
            [jnp.where(even_pair, gath_t, zero), jnp.where(even_pair, zero, gath_t)], axis=1
        ).astype(BF16)

        def near_forward(i, carry):
            part = pl.ds(i * 16, 16)
            lhs = gath[part, :]
            out = jnp.zeros((16, M), F32)
            for j in range(4):
                got = dot_t(lhs, four_blocks(i * 16 + 4 * j))
                got = jnp.where(odd_row, got[:, M:], got[:, :M])
                out = jnp.where(pair_of_row // 2 == j, got, out)
            fwds[part, :] = out
            return carry

        for i in range(12):
            near_forward(i, 0)
        hi, lo = split(fwds[...])
        product = diag_ref[...] * field + spilled[CL : 2 * CL] + dot(hnr_t[...], hi) + dot(hnr_t[...], lo)

        if t < SHORT:
            landed = recv.at[t, pl.ds(0, N - 1)]
            pltpu.make_async_copy(landed, landed, rsem.at[t]).wait()
            arrived = recv[t].reshape(N * ROWS, M)
            if t == 0:
                pick = ones_where(iota((16, M), 1) == iota((16, M), 0))
                numbers = dot_t(pick, arrived)
                col = iota((1, N * ROWS), 1) % ROWS
                first = jnp.concatenate([numbers[:, 3:], numbers[:, :3]], axis=1)
                second = jnp.concatenate([numbers[:, 2:], numbers[:, :2]], axis=1)
                pieces = []
                for q in range(4):
                    number = jnp.where(col == 4, first[q : q + 1], jnp.where(col == 5, second[4 + q : 5 + q], -1.0))
                    pieces.append(ones_where(iota((CL, 1), 0).astype(F32) == number))
                big[pl.ds(FAR, 64), :] = jnp.concatenate(pieces, axis=0)
            got = dot(big[...], arrived)
            totals = got[FAR + 64 : FAR + 65, :]
            totals = totals + pltpu.roll(totals, M - 1, 1) + pltpu.roll(totals, M - 2, 1)
            rw, ww = totals[:, 0:1], totals[:, 3:4]
        else:
            landed = recv4.at[t - SHORT, pl.ds(0, N - 1)]
            pltpu.make_async_copy(landed, landed, rsem.at[t]).wait()
            got = dot(big4[...], recv4[t - SHORT].reshape(N * 4, M))
            landed = sum_b.at[t - SHORT, pl.ds(1, 7)]
            pltpu.make_async_copy(landed, landed, tree_r.at[t - SHORT, 1]).wait()
            totals = jnp.sum(sum_b[t - SHORT], axis=0)
            rw, ww = totals[:, 0:1], totals[:, 1:2]
        c4s[...] = copies(got[0:FAR] * (gmask if t < SHORT else jmask)[...]).astype(BF16)
        if t == 0:
            z = jnp.zeros((CL, R * R), F32)
            for i in range(4):
                part = pl.ds(i * 128, 128)
                c4 = c4s[part, :].astype(F32)
                hi, lo = split(coup[part, :].astype(F32) * jnp.concatenate([c4] * 8, axis=1))
                rows = hrow_t[:, i * 128 : (i + 1) * 128]
                z = z + dot(rows, hi) + dot(rows, lo)
        else:
            z = dot(hrow_t[...], coup[...] * jnp.concatenate([c4s[...]] * 8, axis=1))
        hi, lo = split(z)
        farsum = dot(jnp.concatenate([hi, lo], axis=0), e2_t[...])
        farsum = farsum[0:CL] + farsum[CL:]
        slots = jnp.zeros((CL, M), F32)
        for q in range(4):
            slots = slots + jnp.where(lane // R == q, got[FAR + 16 * q : FAR + 16 * (q + 1), :], 0.0)
        farsum = farsum + copies(slots)
        diag_far = jnp.where(own, jnp.concatenate([farsum] * 4, axis=1), 0.0).astype(BF16)
        product = product + dot(diag_far, basis_ref[...])

        spill_prev.wait_recv()
        spill_next.wait_recv()
        product = product + spin[t, 0] + spin[t, 1]

        if t == 0:
            image = product
        else:
            step = rw / (ww + EPS)
            solution = solution + step * residual
            residual = residual - step * image
            image = image - step * product
        field = image
        if t + 1 < ITERS:
            rw, ww = whole(residual * image), whole(image * image)
            if t + 1 < SHORT:
                sums_tile = to_rows(rw, ww)

    rw, ww = whole(residual * image), whole(image * image)
    last_out[...] = jnp.where(lane == 0, rw, jnp.where(lane == 1, ww, 0.0))
    last_in[me] = last_out[...]

    for there in others:
        pltpu.make_async_remote_copy(
            last_out, last_in.at[me], lsem_s, lsem_r, device_id=there, device_id_type=LOGICAL
        ).start()
    everyone = last_in.at[pl.ds(0, N - 1)]
    pltpu.make_async_copy(everyone, everyone, lsem_r).wait()
    totals = jnp.sum(last_in[...], axis=0)
    step = totals[:, 0:1] / (totals[:, 1:2] + EPS)
    out_ref[0] = solution
    out_ref[1] = residual
    out_ref[2] = image
    out_ref[3] = jnp.broadcast_to(step, (CL, M))

    pltpu.make_async_copy(everyone, everyone, lsem_s).wait()
    for t in range(ITERS - SHORT):
        sent = sum_a.at[t, pl.ds(1, 15)]
        pltpu.make_async_copy(sent, sent, tree_s.at[t, 0]).wait()
        sent = sum_b.at[t, pl.ds(1, 7)]
        pltpu.make_async_copy(sent, sent, tree_s.at[t, 1]).wait()
    for t in range(ITERS):
        sent = send.at[t, pl.ds(0, N - 1)] if t < SHORT else send4.at[t - SHORT, pl.ds(0, N - 1)]
        pltpu.make_async_copy(sent, sent, ssem.at[t]).wait()
        for i in range(2):
            pltpu.make_async_copy(win.at[t, 1], win.at[t, 1], wsem_s.at[t, i]).wait()
            pltpu.make_async_copy(spout.at[t, i], spout.at[t, i], psem_s.at[t, i]).wait()


def on_device(rs, diag, near, nrow, ncol, ncount, basis, coup, frow, fcol, frank):
    vmem = pl.BlockSpec(memory_space=pltpu.VMEM)
    hbm = pl.BlockSpec(memory_space=pl.ANY)
    ints = jnp.int32
    v = pltpu.VMEM
    dma = pltpu.SemaphoreType.DMA
    out = pl.pallas_call(
        kernel,
        out_shape=jax.ShapeDtypeStruct((4, CL, M), F32),
        in_specs=[hbm] * 12,
        out_specs=vmem,
        scratch_shapes=[
            v((CL, M), F32),
            v((CL, M), F32),
            v((1, NEAR), ints),
            v((1, NEAR), ints),
            pltpu.SMEM((1, 1), ints),
            v((CL * R, M), BF16),
            v((1, FAR), ints),
            v((1, FAR), ints),
            v((1, FAR), ints),
            v((8, N * (ROWS + 4)), ints),
            v((NEAR, M, M), BF16),
            v((FAR, R * R), BF16),
            v((FAR, R * R), BF16),
            v((FAR + 80, N * ROWS), BF16),
            v((N * ROWS, FAR), BF16),
            v((R * R, M), BF16),
            v((M, CL * R), BF16),
            v((FAR, CL), BF16),
            v((CL, FAR), BF16),
            v((FAR, M), F32),
            v((FAR, M), F32),
            v((NEAR, CL), BF16),
            v((NEAR, 3 * CL), BF16),
            v((CL, NEAR), BF16),
            v((3 * CL, NEAR), BF16),
            v((N * ROWS, M), F32),
            v((FAR + 64, N * 4), BF16),
            v((N * 4, FAR), BF16),
            v((N * 4, M), BF16),
            v((ITERS - SHORT, N, 4, M), BF16),
            v((ITERS - SHORT, N, 4, M), BF16),
            v((ITERS - SHORT, 1, M), F32),
            v((ITERS - SHORT, 16, 1, M), F32),
            v((ITERS - SHORT, 1, M), F32),
            v((ITERS - SHORT, 8, 1, M), F32),
            dma((ITERS - SHORT, 2)),
            dma((ITERS - SHORT, 2)),
            v((NEAR, 2 * M), BF16),
            v((NEAR, 2 * M), BF16),
            v((NEAR, M), F32),
            v((NEAR, M), F32),
            v((FAR, M), BF16),
            v((SHORT, N, ROWS, M), BF16),
            v((SHORT, N, ROWS, M), BF16),
            v((ITERS, 3, CL, M), BF16),
            v((ITERS, 2, CL, M), F32),
            v((ITERS, 2, CL, M), F32),
            v((1, M), F32),
            v((N, 1, M), F32),
            dma((12,)),
            dma((ITERS,)),
            dma((ITERS,)),
            dma((ITERS, 2)),
            dma((ITERS, 2)),
            dma((ITERS, 2)),
            dma((ITERS, 2)),
            dma,
            dma,
        ],
        compiler_params=pltpu.CompilerParams(
            collective_id=0, has_side_effects=True, vmem_limit_bytes=60 << 20
        ),
    )(
        rs,
        diag,
        near,
        nrow.reshape(1, NEAR),
        ncol.reshape(1, NEAR),
        ncount.reshape(1, 1),
        basis.reshape(CL * R, M),
        coup,
        frow.reshape(1, FAR),
        fcol.reshape(1, FAR),
        frank.reshape(1, FAR),
        jnp.asarray(order_table()),
    )
    return out[0] + out[3] * out[1], out[1] - out[3] * out[2]


def solution(mesh):
    flat = P(AXES)
    two = P(AXES, None)
    three = P(AXES, None, None)
    return jax.shard_map(
        on_device,
        mesh=mesh,
        in_specs=(two, two, three, flat, flat, flat, three, two, flat, flat, flat),
        out_specs=(two, two),
        check_vma=False,
    )
```

```python
import functools

import jax
import jax.numpy as jnp
import numpy as np
from jax import lax
from jax.experimental import pallas as pl
from jax.experimental.pallas import tpu as pltpu
from jax.sharding import PartitionSpec as P

ITERS = 3
AXES = ("gx", "gy", "gz")
N = 128
CL = 16
M = 128
R = 32
NEAR = 192
FAR = 512
ROWS = 8
EPS = 1e-6
F32, BF16 = jnp.float32, jnp.bfloat16
LOGICAL = pl.DeviceIdType.LOGICAL


STEPS = sorted(
    ((code, core) for code in range(64) for core in range(2) if (code, core) != (0, 0)),
    key=lambda s: (-bin(s[0]).count("1"), s[0], s[1]),
)
GRAY = (0, 1, 3, 2)
SHORT = 1
PLANE = sorted(range(1, 16), key=lambda o: -min(o // 4, 4 - o // 4) - min(o % 4, 4 - o % 4))
FIRST = 48
NEXT = 6
PLACE = {step: i for i, step in enumerate(STEPS)}
BACK = [
    PLACE[(sum((0, 2, 1, 3)[code >> shift & 3] << shift for shift in (0, 2, 4)), core)] for code, core in STEPS
]


def order_table():
    steps = STEPS + [(0, 0)]
    table = np.zeros((8, N * (ROWS + 4)), np.int32)
    for i, (code, core) in enumerate(steps):
        for part in (slice(i * ROWS, (i + 1) * ROWS), slice(N * ROWS + i * 4, N * ROWS + (i + 1) * 4)):
            table[0, part] = GRAY[code // 16]
            table[1, part] = core
            table[2, part] = GRAY[code // 4 % 4]
            table[3, part] = GRAY[code % 4]
    return table


def partners():
    gx, gy, gz = lax.axis_index("gx"), lax.axis_index("gy"), lax.axis_index("gz")
    x, core = gx // 2, gx % 2
    xs = [((x + step) % 4) * 32 for step in range(4)]
    cores = [core * 16, (1 - core) * 16]
    zs = [((gy + step) % 4) * 4 for step in range(4)]
    ys = [(gz + step) % 4 for step in range(4)]
    return [
        xs[GRAY[code // 16]] + cores[other] + zs[GRAY[code // 4 % 4]] + ys[GRAY[code % 4]] for code, other in STEPS
    ]


def iota(shape, dim):
    return lax.broadcasted_iota(jnp.int32, shape, dim)


def ones_where(cond):
    return jnp.where(cond, 1.0, 0.0).astype(BF16)


def dot(a, b):
    return jnp.dot(a, b, preferred_element_type=F32)


def dot_t(a, b):
    return lax.dot_general(a, b, (((1,), (1,)), ((), ())), preferred_element_type=F32)


def copies(x):
    x = x + pltpu.roll(x, 2 * R, 1)
    return x + pltpu.roll(x, R, 1)


def whole(x):
    return jnp.sum(jnp.sum(x, axis=0, keepdims=True), axis=1, keepdims=True)


def split(x):
    hi = x.astype(BF16)
    return hi, (x - hi.astype(F32)).astype(BF16)


def kernel(
    rs_hbm, diag_hbm, near_hbm, nrow_hbm, ncol_hbm, ncount_hbm, basis_hbm, coup_hbm, frow_hbm, fcol_hbm, frank_hbm, table_hbm,
    out_ref,
    rs_ref, diag_ref, nrow_ref, ncol_ref, ncount_ref, basis_ref, frow_ref, fcol_ref, frank_ref, table_ref,
    near, coup, coup_t, big, t8, e2_t, basis_t, hrow, hrow_t, gmask, jmask, hnr, hnc, hnr_t, hnc_t, meta,
    big4, t4, pick4, repeat4, send4, recv4, sum_out, sum_a, sum_mid, sum_b, tree_s, tree_r, gath, grow, backs, fwds, c4s, send, recv, win, spout, spin, last_out, last_in,
    dma_sem, ssem, rsem, wsem_s, wsem_r, psem_s, psem_r, lsem_s, lsem_r,
):
    me = lax.axis_index(AXES)
    nxt, prv = lax.rem(me + 1, N), lax.rem(me + N - 1, N)
    load_coup = pltpu.make_async_copy(coup_hbm, coup, dma_sem.at[0])
    load_near = pltpu.make_async_copy(near_hbm, near, dma_sem.at[1])
    pairs = (
        (frow_hbm, frow_ref), (fcol_hbm, fcol_ref), (frank_hbm, frank_ref), (nrow_hbm, nrow_ref), (ncol_hbm, ncol_ref),
        (ncount_hbm, ncount_ref), (rs_hbm, rs_ref), (basis_hbm, basis_ref), (diag_hbm, diag_ref), (table_hbm, table_ref),
    )
    loads = [pltpu.make_async_copy(a, b, dma_sem.at[2 + i]) for i, (a, b) in enumerate(pairs)]
    for load in loads:
        load.start()
    load_coup.start()
    load_near.start()

    barrier = pltpu.get_barrier_semaphore()

    others = partners()
    for there in others:
        pl.semaphore_signal(barrier, inc=1, device_id=there, device_id_type=LOGICAL)
    for load in loads:
        load.wait()

    frow = frow_ref[...] - me * CL
    fcol = fcol_ref[...]
    owner = fcol // CL
    local = fcol - owner * CL
    rank = frank_ref[...]
    owner_f = owner.astype(F32)
    codes = jnp.concatenate(
        [frow.astype(F32), owner_f, local.astype(F32), rank.astype(F32), jnp.zeros((4, FAR), F32)], axis=0
    )
    codes_t = jnp.transpose(codes)
    frow_c = codes_t[:, 0:1].astype(jnp.int32)
    owner_c = codes_t[:, 1:2].astype(jnp.int32)
    local_c = codes_t[:, 2:3].astype(jnp.int32)
    rank_c = codes_t[:, 3:4].astype(jnp.int32)
    same = jnp.where((owner_c == owner) & (iota((FAR, FAR), 0) < iota((FAR, FAR), 1)), 1.0, 0.0)
    place_f = jnp.sum(same, axis=0, keepdims=True)
    place = place_f.astype(jnp.int32)
    place_c = jnp.transpose(jnp.broadcast_to(place_f, (8, FAR)))[:, 0:1].astype(jnp.int32)

    lane = iota((1, M), 1)
    gmask[...] = jnp.where(lane // R == local_c % 4, 1.0, 0.0)
    jmask[...] = jnp.where(lane // R == place_c % 4, 1.0, 0.0)
    hrow[...] = ones_where(iota((1, CL), 1) == frow_c)
    hrow_t[...] = ones_where(iota((CL, 1), 0) == frow)
    code_g = owner_c * ROWS + local_c // 4
    gx, gy, gz = lax.axis_index("gx"), lax.axis_index("gy"), lax.axis_index("gz")
    repeat4[...] = ones_where(iota((N * 4, N), 0) // 4 == iota((N * 4, N), 1))
    steps = table_ref[...]
    source = (
        (gx // 2 + steps[0:1]) % 4 * 32 + (gx % 2 + steps[1:2]) % 2 * 16 + (gy + steps[2:3]) % 4 * 4 + (gz + steps[3:4]) % 4
    )
    big[pl.ds(0, FAR), :] = ones_where(source[:, 0 : N * ROWS] * ROWS + iota((1, N * ROWS), 1) % ROWS == code_g)
    source4 = source[:, N * ROWS :]
    big4[pl.ds(0, FAR), :] = ones_where(source4 * 4 + iota((1, N * 4), 1) % 4 == owner_c * 4 + place_c // 4)
    source4_c = jnp.transpose(jnp.broadcast_to(source4.astype(F32), (8, N * 4)))[:, 0:1].astype(jnp.int32)
    row4 = iota((N * 4, 1), 0) % 4
    t4[...] = ones_where(source4_c * 4 + row4 == owner * 4 + 2 + place // 4)
    code_s = owner * ROWS + 4 + place // 4
    t8[...] = ones_where(iota((N * ROWS, 1), 0) == code_s)
    e2_t[...] = ones_where(iota((R * R, M), 0) // R == iota((R * R, M), 1) % R)
    eye = ones_where(iota((M, M), 0) == iota((M, M), 1))
    basis_t[...] = dot_t(eye, basis_ref[...]).astype(BF16)
    code_m = owner * ROWS + 7
    t7 = ones_where(iota((N * ROWS, 1), 0) == code_m)
    meta[...] = dot(t7, jnp.where(lane == place_c, local_c.astype(F32), 0.0).astype(BF16))
    count = ncount_ref[0, 0]
    live = iota((1, NEAR), 1) < count
    nrow = nrow_ref[...] - me * CL
    ncol = ncol_ref[...] - me * CL + CL
    hnr_t[...] = ones_where((iota((CL, 1), 0) == nrow) & live)
    hnc_t[...] = ones_where((iota((3 * CL, 1), 0) == ncol) & live)
    ncodes = jnp.concatenate([nrow.astype(F32), ncol.astype(F32), jnp.zeros((6, NEAR), F32)], axis=0)
    ncodes_t = jnp.transpose(ncodes)
    hnr[...] = ones_where(iota((1, CL), 1) == ncodes_t[:, 0:1].astype(jnp.int32))
    hnc[...] = ones_where(iota((1, 3 * CL), 1) == ncodes_t[:, 1:2].astype(jnp.int32))

    load_coup.wait()
    ab = iota((1, R * R), 1)
    top = jnp.maximum(ab // R, ab % R)
    coup[...] = jnp.where(top < rank_c, coup[...].astype(F32), 0.0).astype(BF16)
    flip = ones_where(iota((R * R, 1), 0) == (ab % R) * R + ab // R)
    for i in range(4):
        part = pl.ds(i * 128, 128)
        coup_t[part, :] = dot(coup[part, :], flip).astype(BF16)

    own = iota((CL, CL * R), 1) // R == iota((CL, CL * R), 0)
    rows_of = ones_where(iota((ROWS, CL), 1) // 4 == iota((ROWS, CL), 0))
    even = iota((NEAR, 1), 0) % 2 == 0
    even_pair = iota((NEAR, 1), 0) % 4 < 2

    def four_blocks(k):
        first = near[pl.ds(k, 2)].reshape(2 * M, M)
        second = near[pl.ds(k + 2, 2)].reshape(2 * M, M)
        return jnp.concatenate([first, second], axis=1)

    pair_of_row = iota((16, 1), 0) // 2
    odd_row = iota((16, 1), 0) % 2 == 1

    field = rs_ref[...]
    residual = field
    solution = jnp.zeros_like(field)
    image = field

    for t in range(ITERS):
        low = field.astype(BF16)
        if t >= SHORT:
            sum_out[t - SHORT] = jnp.where(lane == 0, rw, jnp.where(lane == 1, ww, 0.0))
            sum_a[t - SHORT, 0] = sum_out[t - SHORT]
            for o in PLANE:
                pltpu.make_async_remote_copy(
                    sum_out.at[t - SHORT], sum_a.at[t - SHORT, o], tree_s.at[t - SHORT, 0], tree_r.at[t - SHORT, 0],
                    device_id=gx * 16 + (gy + o // 4) % 4 * 4 + (gz + o % 4) % 4, device_id_type=LOGICAL,
                ).start()
        win[t, 1] = low
        if t == 0:
            pl.semaphore_wait(barrier, N - 1)
        to_next = pltpu.make_async_remote_copy(
            win.at[t, 1], win.at[t, 0], wsem_s.at[t, 0], wsem_r.at[t, 0], device_id=nxt, device_id_type=LOGICAL
        )
        to_prev = pltpu.make_async_remote_copy(
            win.at[t, 1], win.at[t, 2], wsem_s.at[t, 1], wsem_r.at[t, 1], device_id=prv, device_id_type=LOGICAL
        )
        to_next.start()
        to_prev.start()

        raw = jnp.where(own, dot(low, basis_t[...]), 0.0)
        coeffs = (raw[:, 0:M] + raw[:, M : 2 * M] + raw[:, 2 * M : 3 * M] + raw[:, 3 * M : 4 * M]).astype(BF16)
        four = copies(coeffs.astype(F32))
        wide = dot(hrow[...], four.astype(BF16)).astype(BF16)
        if t == 0:
            for i in range(4):
                part = pl.ds(i * 128, 128)
                prods = coup_t[part, :].astype(F32) * jnp.concatenate([wide[i * 128 : (i + 1) * 128].astype(F32)] * 8, axis=1)
                hi, lo = split(prods)
                c4s[part, :] = ((dot(hi, e2_t[...]) + dot(lo, e2_t[...])) * jmask[part, :]).astype(BF16)
        else:
            prods = coup_t[...] * jnp.concatenate([wide] * 8, axis=1)
            c4s[...] = (dot(prods, e2_t[...]) * jmask[...]).astype(BF16)
        if t < SHORT:
            message = dot(t8[...], c4s[...])
            tile = dot(rows_of, coeffs)
            if t == 0:
                message = message + meta[...]
            send[t] = (message.reshape(N, ROWS, M) + tile[None]).astype(BF16)
            recv[t, N - 1] = send[t, me]
        else:
            spread4 = jnp.concatenate([jnp.where(lane // R == q, four, 0.0) for q in range(4)] + [jnp.zeros((64, M), F32)], axis=0)
            message = dot(t4[...], c4s[...]) + dot(pick4[...], spread4.astype(BF16))
            send4[t - SHORT] = message.reshape(N, 4, M).astype(BF16)
            recv4[t - SHORT, N - 1] = send4[t - SHORT, N - 1]

        grow_t = dot(hnr[...], low)
        zero = jnp.zeros_like(grow_t)
        grow[...] = jnp.concatenate([jnp.where(even, grow_t, zero), jnp.where(even, zero, grow_t)], axis=1).astype(BF16)

        def far_send(i, t=t):
            there = others[i]
            if t < SHORT:
                src, dst = send.at[t, there], recv.at[t, BACK[i]]
            else:
                src, dst = send4.at[t - SHORT, i], recv4.at[t - SHORT, BACK[i]]
            pltpu.make_async_remote_copy(
                src, dst, ssem.at[t], rsem.at[t], device_id=there, device_id_type=LOGICAL
            ).start()

        for i in range(N - 1):
            far_send(i)

        if t == 0:
            load_near.wait()

        def near_back(i, carry):
            part = pl.ds(i * 16, 16)
            lhs = grow[part, :]
            out = jnp.zeros((16, M), F32)
            for j in range(4):
                out_j = dot(lhs, four_blocks(i * 16 + 4 * j))
                out = jnp.where(pair_of_row == 2 * j, out_j[:, :M], out)
                out = jnp.where(pair_of_row == 2 * j + 1, out_j[:, M:], out)
            backs[part, :] = out
            return carry

        for i in range(12):
            near_back(i, 0)
        hi, lo = split(backs[...])
        spilled = dot(hnc_t[...], hi) + dot(hnc_t[...], lo)
        spout[t, 0] = spilled[0:CL]
        spout[t, 1] = spilled[2 * CL : 3 * CL]
        spill_prev = pltpu.make_async_remote_copy(
            spout.at[t, 0], spin.at[t, 1], psem_s.at[t, 0], psem_r.at[t, 1], device_id=prv, device_id_type=LOGICAL
        )
        spill_next = pltpu.make_async_remote_copy(
            spout.at[t, 1], spin.at[t, 0], psem_s.at[t, 1], psem_r.at[t, 0], device_id=nxt, device_id_type=LOGICAL
        )
        spill_prev.start()
        spill_next.start()
        if t >= SHORT:
            landed = sum_a.at[t - SHORT, pl.ds(1, 15)]
            pltpu.make_async_copy(landed, landed, tree_r.at[t - SHORT, 0]).wait()
            sum_mid[t - SHORT] = jnp.sum(sum_a[t - SHORT], axis=0)
            sum_b[t - SHORT, 0] = sum_mid[t - SHORT]
            for o in (4, 5, 2, 3, 6, 7, 1):
                pltpu.make_async_remote_copy(
                    sum_mid.at[t - SHORT], sum_b.at[t - SHORT, o], tree_s.at[t - SHORT, 1], tree_r.at[t - SHORT, 1],
                    device_id=(gx + o) % 8 * 16 + gy * 4 + gz, device_id_type=LOGICAL,
                ).start()

        to_next.wait_recv()
        to_prev.wait_recv()
        gath_t = dot(hnc[...], win[t].reshape(3 * CL, M))
        gath[...] = jnp.concatenate(
            [jnp.where(even_pair, gath_t, zero), jnp.where(even_pair, zero, gath_t)], axis=1
        ).astype(BF16)

        def near_forward(i, carry):
            part = pl.ds(i * 16, 16)
            lhs = gath[part, :]
            out = jnp.zeros((16, M), F32)
            for j in range(4):
                got = dot_t(lhs, four_blocks(i * 16 + 4 * j))
                got = jnp.where(odd_row, got[:, M:], got[:, :M])
                out = jnp.where(pair_of_row // 2 == j, got, out)
            fwds[part, :] = out
            return carry

        for i in range(12):
            near_forward(i, 0)
        hi, lo = split(fwds[...])
        product = diag_ref[...] * field + spilled[CL : 2 * CL] + dot(hnr_t[...], hi) + dot(hnr_t[...], lo)

        if t < SHORT:
            landed = recv.at[t, pl.ds(0, N - 1)]
            pltpu.make_async_copy(landed, landed, rsem.at[t]).wait()
            arrived = recv[t].reshape(N * ROWS, M)
            if t == 0:
                pick = ones_where(iota((16, M), 1) == iota((16, M), 0))
                numbers = dot_t(pick, arrived)
                col = iota((1, N * ROWS), 1) % ROWS
                first = jnp.concatenate([numbers[:, 3:], numbers[:, :3]], axis=1)
                second = jnp.concatenate([numbers[:, 2:], numbers[:, :2]], axis=1)
                pieces = []
                for q in range(4):
                    number = jnp.where(col == 4, first[q : q + 1], jnp.where(col == 5, second[4 + q : 5 + q], -1.0))
                    pieces.append(ones_where(iota((CL, 1), 0).astype(F32) == number))
                big[pl.ds(FAR, 64), :] = jnp.concatenate(pieces, axis=0)
            got = dot(big[...], arrived)
            numbers = dot(repeat4[...], recv[0].astype(F32)[:, 7, :].astype(BF16))
            numbers = jnp.where(row4 % 2 == 0, numbers, pltpu.roll(numbers, M - 4, 1))
            spread = ones_where((iota((M, M), 0) == iota((M, M), 1) // CL) & (iota((M, M), 0) < 4))
            numbers = dot(numbers.astype(BF16), spread)
            hot = jnp.where((iota((1, M), 1) % CL).astype(F32) == numbers, 1.0, 0.0)
            hot = jnp.where(iota((1, M), 1) < 64, hot, 0.0)
            pick4[...] = jnp.where(row4 < 2, hot, 0.0).astype(BF16)
            big4[pl.ds(FAR, 64), :] = jnp.transpose(jnp.where(row4 >= 2, hot, 0.0))[0:64, :].astype(BF16)
        else:
            landed = recv4.at[t - SHORT, pl.ds(0, N - 1)]
            pltpu.make_async_copy(landed, landed, rsem.at[t]).wait()
            got = dot(big4[...], recv4[t - SHORT].reshape(N * 4, M))
            landed = sum_b.at[t - SHORT, pl.ds(1, 7)]
            pltpu.make_async_copy(landed, landed, tree_r.at[t - SHORT, 1]).wait()
            totals = jnp.sum(sum_b[t - SHORT], axis=0)
            rw, ww = totals[:, 0:1], totals[:, 1:2]
        c4s[...] = copies(got[0:FAR] * (gmask if t < SHORT else jmask)[...]).astype(BF16)
        if t == 0:
            z = jnp.zeros((CL, R * R), F32)
            for i in range(4):
                part = pl.ds(i * 128, 128)
                c4 = c4s[part, :].astype(F32)
                hi, lo = split(coup[part, :].astype(F32) * jnp.concatenate([c4] * 8, axis=1))
                rows = hrow_t[:, i * 128 : (i + 1) * 128]
                z = z + dot(rows, hi) + dot(rows, lo)
        else:
            z = dot(hrow_t[...], coup[...] * jnp.concatenate([c4s[...]] * 8, axis=1))
        hi, lo = split(z)
        farsum = dot(jnp.concatenate([hi, lo], axis=0), e2_t[...])
        farsum = farsum[0:CL] + farsum[CL:]
        slots = jnp.zeros((CL, M), F32)
        for q in range(4):
            slots = slots + jnp.where(lane // R == q, got[FAR + 16 * q : FAR + 16 * (q + 1), :], 0.0)
        farsum = farsum + copies(slots)
        diag_far = jnp.where(own, jnp.concatenate([farsum] * 4, axis=1), 0.0).astype(BF16)
        product = product + dot(diag_far, basis_ref[...])

        spill_prev.wait_recv()
        spill_next.wait_recv()
        product = product + spin[t, 0] + spin[t, 1]

        if t == 0:
            image = product
        else:
            step = rw / (ww + EPS)
            solution = solution + step * residual
            residual = residual - step * image
            image = image - step * product
        field = image
        if t + 1 < ITERS:
            rw, ww = whole(residual * image), whole(image * image)

    rw, ww = whole(residual * image), whole(image * image)
    last_out[...] = jnp.where(lane == 0, rw, jnp.where(lane == 1, ww, 0.0))
    last_in[me] = last_out[...]

    for there in others:
        pltpu.make_async_remote_copy(
            last_out, last_in.at[me], lsem_s, lsem_r, device_id=there, device_id_type=LOGICAL
        ).start()
    everyone = last_in.at[pl.ds(0, N - 1)]
    pltpu.make_async_copy(everyone, everyone, lsem_r).wait()
    totals = jnp.sum(last_in[...], axis=0)
    step = totals[:, 0:1] / (totals[:, 1:2] + EPS)
    out_ref[0] = solution
    out_ref[1] = residual
    out_ref[2] = image
    out_ref[3] = jnp.broadcast_to(step, (CL, M))

    pltpu.make_async_copy(everyone, everyone, lsem_s).wait()
    for t in range(ITERS - SHORT):
        sent = sum_a.at[t, pl.ds(1, 15)]
        pltpu.make_async_copy(sent, sent, tree_s.at[t, 0]).wait()
        sent = sum_b.at[t, pl.ds(1, 7)]
        pltpu.make_async_copy(sent, sent, tree_s.at[t, 1]).wait()
    for t in range(ITERS):
        sent = send.at[t, pl.ds(0, N - 1)] if t < SHORT else send4.at[t - SHORT, pl.ds(0, N - 1)]
        pltpu.make_async_copy(sent, sent, ssem.at[t]).wait()
        for i in range(2):
            pltpu.make_async_copy(win.at[t, 1], win.at[t, 1], wsem_s.at[t, i]).wait()
            pltpu.make_async_copy(spout.at[t, i], spout.at[t, i], psem_s.at[t, i]).wait()


def on_device(rs, diag, near, nrow, ncol, ncount, basis, coup, frow, fcol, frank):
    vmem = pl.BlockSpec(memory_space=pltpu.VMEM)
    hbm = pl.BlockSpec(memory_space=pl.ANY)
    ints = jnp.int32
    v = pltpu.VMEM
    dma = pltpu.SemaphoreType.DMA
    out = pl.pallas_call(
        kernel,
        out_shape=jax.ShapeDtypeStruct((4, CL, M), F32),
        in_specs=[hbm] * 12,
        out_specs=vmem,
        scratch_shapes=[
            v((CL, M), F32),
            v((CL, M), F32),
            v((1, NEAR), ints),
            v((1, NEAR), ints),
            pltpu.SMEM((1, 1), ints),
            v((CL * R, M), BF16),
            v((1, FAR), ints),
            v((1, FAR), ints),
            v((1, FAR), ints),
            v((8, N * (ROWS + 4)), ints),
            v((NEAR, M, M), BF16),
            v((FAR, R * R), BF16),
            v((FAR, R * R), BF16),
            v((FAR + 64, N * ROWS), BF16),
            v((N * ROWS, FAR), BF16),
            v((R * R, M), BF16),
            v((M, CL * R), BF16),
            v((FAR, CL), BF16),
            v((CL, FAR), BF16),
            v((FAR, M), F32),
            v((FAR, M), F32),
            v((NEAR, CL), BF16),
            v((NEAR, 3 * CL), BF16),
            v((CL, NEAR), BF16),
            v((3 * CL, NEAR), BF16),
            v((N * ROWS, M), F32),
            v((FAR + 64, N * 4), BF16),
            v((N * 4, FAR), BF16),
            v((N * 4, M), BF16),
            v((N * 4, N), BF16),
            v((ITERS - SHORT, N, 4, M), BF16),
            v((ITERS - SHORT, N, 4, M), BF16),
            v((ITERS - SHORT, 1, M), F32),
            v((ITERS - SHORT, 16, 1, M), F32),
            v((ITERS - SHORT, 1, M), F32),
            v((ITERS - SHORT, 8, 1, M), F32),
            dma((ITERS - SHORT, 2)),
            dma((ITERS - SHORT, 2)),
            v((NEAR, 2 * M), BF16),
            v((NEAR, 2 * M), BF16),
            v((NEAR, M), F32),
            v((NEAR, M), F32),
            v((FAR, M), BF16),
            v((SHORT, N, ROWS, M), BF16),
            v((SHORT, N, ROWS, M), BF16),
            v((ITERS, 3, CL, M), BF16),
            v((ITERS, 2, CL, M), F32),
            v((ITERS, 2, CL, M), F32),
            v((1, M), F32),
            v((N, 1, M), F32),
            dma((12,)),
            dma((ITERS,)),
            dma((ITERS,)),
            dma((ITERS, 2)),
            dma((ITERS, 2)),
            dma((ITERS, 2)),
            dma((ITERS, 2)),
            dma,
            dma,
        ],
        compiler_params=pltpu.CompilerParams(
            collective_id=0, has_side_effects=True, vmem_limit_bytes=60 << 20
        ),
    )(
        rs,
        diag,
        near,
        nrow.reshape(1, NEAR),
        ncol.reshape(1, NEAR),
        ncount.reshape(1, 1),
        basis.reshape(CL * R, M),
        coup,
        frow.reshape(1, FAR),
        fcol.reshape(1, FAR),
        frank.reshape(1, FAR),
        jnp.asarray(order_table()),
    )
    return out[0] + out[3] * out[1], out[1] - out[3] * out[2]


def solution(mesh):
    flat = P(AXES)
    two = P(AXES, None)
    three = P(AXES, None, None)
    return jax.shard_map(
        on_device,
        mesh=mesh,
        in_specs=(two, two, three, flat, flat, flat, three, two, flat, flat, flat),
        out_specs=(two, two),
        check_vma=False,
    )
```

```python
import functools

import jax
import jax.numpy as jnp
import numpy as np
from jax import lax
from jax.experimental import pallas as pl
from jax.experimental.pallas import tpu as pltpu
from jax.sharding import PartitionSpec as P

ITERS = 3
AXES = ("gx", "gy", "gz")
N = 128
CL = 16
M = 128
R = 32
NEAR = 192
FAR = 512
ROWS = 8
EPS = 1e-6
F32, BF16 = jnp.float32, jnp.bfloat16
LOGICAL = pl.DeviceIdType.LOGICAL


STEPS = sorted(
    ((code, core) for code in range(64) for core in range(2) if (code, core) != (0, 0)),
    key=lambda s: (-bin(s[0]).count("1"), s[0], s[1]),
)
GRAY = (0, 1, 3, 2)
SHORT = 1
PLANE = sorted(range(1, 16), key=lambda o: -min(o // 4, 4 - o // 4) - min(o % 4, 4 - o % 4))
FIRST = 48
NEXT = 6
PLACE = {step: i for i, step in enumerate(STEPS)}
BACK = [
    PLACE[(sum((0, 2, 1, 3)[code >> shift & 3] << shift for shift in (0, 2, 4)), core)] for code, core in STEPS
]


def order_table():
    steps = STEPS + [(0, 0)]
    table = np.zeros((8, N * (ROWS + 4)), np.int32)
    for i, (code, core) in enumerate(steps):
        for part in (slice(i * ROWS, (i + 1) * ROWS), slice(N * ROWS + i * 4, N * ROWS + (i + 1) * 4)):
            table[0, part] = GRAY[code // 16]
            table[1, part] = core
            table[2, part] = GRAY[code // 4 % 4]
            table[3, part] = GRAY[code % 4]
    return table


def partners():
    gx, gy, gz = lax.axis_index("gx"), lax.axis_index("gy"), lax.axis_index("gz")
    x, core = gx // 2, gx % 2
    xs = [((x + step) % 4) * 32 for step in range(4)]
    cores = [core * 16, (1 - core) * 16]
    zs = [((gy + step) % 4) * 4 for step in range(4)]
    ys = [(gz + step) % 4 for step in range(4)]
    return [
        xs[GRAY[code // 16]] + cores[other] + zs[GRAY[code // 4 % 4]] + ys[GRAY[code % 4]] for code, other in STEPS
    ]


def iota(shape, dim):
    return lax.broadcasted_iota(jnp.int32, shape, dim)


def ones_where(cond):
    return jnp.where(cond, 1.0, 0.0).astype(BF16)


def dot(a, b):
    return jnp.dot(a, b, preferred_element_type=F32)


def dot_t(a, b):
    return lax.dot_general(a, b, (((1,), (1,)), ((), ())), preferred_element_type=F32)


def copies(x):
    x = x + pltpu.roll(x, 2 * R, 1)
    return x + pltpu.roll(x, R, 1)


def whole(x):
    return jnp.sum(jnp.sum(x, axis=0, keepdims=True), axis=1, keepdims=True)


def split(x):
    hi = x.astype(BF16)
    return hi, (x - hi.astype(F32)).astype(BF16)


def kernel(
    rs_hbm, diag_hbm, near_hbm, nrow_hbm, ncol_hbm, ncount_hbm, basis_hbm, coup_hbm, frow_hbm, fcol_hbm, frank_hbm, table_hbm,
    out_ref,
    rs_ref, diag_ref, nrow_ref, ncol_ref, ncount_ref, basis_ref, frow_ref, fcol_ref, frank_ref, table_ref,
    near, coup, coup_t, big, t8, e2_t, basis_t, hrow, hrow_t, gmask, jmask, hnr, hnc, hnr_t, hnc_t, meta,
    big4, t4, pick4, repeat4, send4, recv4, sum_out, sum_a, sum_mid, sum_b, tree_s, tree_r, gath, grow, backs, fwds, c4s, send, recv, win, spout, spin, last_out, last_in,
    dma_sem, ssem, rsem, wsem_s, wsem_r, psem_s, psem_r, lsem_s, lsem_r,
):
    me = lax.axis_index(AXES)
    nxt, prv = lax.rem(me + 1, N), lax.rem(me + N - 1, N)
    load_coup = pltpu.make_async_copy(coup_hbm, coup, dma_sem.at[0])
    load_near = pltpu.make_async_copy(near_hbm, near, dma_sem.at[1])
    pairs = (
        (frow_hbm, frow_ref), (fcol_hbm, fcol_ref), (frank_hbm, frank_ref), (nrow_hbm, nrow_ref), (ncol_hbm, ncol_ref),
        (ncount_hbm, ncount_ref), (rs_hbm, rs_ref), (basis_hbm, basis_ref), (diag_hbm, diag_ref), (table_hbm, table_ref),
    )
    loads = [pltpu.make_async_copy(a, b, dma_sem.at[2 + i]) for i, (a, b) in enumerate(pairs)]
    for load in loads:
        load.start()
    load_coup.start()
    load_near.start()

    barrier = pltpu.get_barrier_semaphore()

    others = partners()
    for there in others:
        pl.semaphore_signal(barrier, inc=1, device_id=there, device_id_type=LOGICAL)
    for load in loads:
        load.wait()

    frow = frow_ref[...] - me * CL
    fcol = fcol_ref[...]
    owner = fcol // CL
    local = fcol - owner * CL
    rank = frank_ref[...]
    owner_f = owner.astype(F32)
    codes = jnp.concatenate(
        [frow.astype(F32), owner_f, local.astype(F32), rank.astype(F32), jnp.zeros((4, FAR), F32)], axis=0
    )
    codes_t = jnp.transpose(codes)
    frow_c = codes_t[:, 0:1].astype(jnp.int32)
    owner_c = codes_t[:, 1:2].astype(jnp.int32)
    local_c = codes_t[:, 2:3].astype(jnp.int32)
    rank_c = codes_t[:, 3:4].astype(jnp.int32)
    same = jnp.where((owner_c == owner) & (iota((FAR, FAR), 0) < iota((FAR, FAR), 1)), 1.0, 0.0)
    place_f = jnp.sum(same, axis=0, keepdims=True)
    place = place_f.astype(jnp.int32)
    place_c = jnp.transpose(jnp.broadcast_to(place_f, (8, FAR)))[:, 0:1].astype(jnp.int32)

    lane = iota((1, M), 1)
    jmask[...] = jnp.where(lane // R == place_c % 4, 1.0, 0.0)
    hrow[...] = ones_where(iota((1, CL), 1) == frow_c)
    code_s = owner * ROWS + 4 + place // 4
    t8[...] = ones_where(iota((N * ROWS, 1), 0) == code_s)
    e2_t[...] = ones_where(iota((R * R, M), 0) // R == iota((R * R, M), 1) % R)
    eye = ones_where(iota((M, M), 0) == iota((M, M), 1))
    basis_t[...] = dot_t(eye, basis_ref[...]).astype(BF16)
    code_m = owner * ROWS + 7
    t7 = ones_where(iota((N * ROWS, 1), 0) == code_m)
    meta[...] = dot(t7, jnp.where(lane == place_c, local_c.astype(F32), 0.0).astype(BF16))
    row4 = iota((N * 4, 1), 0) % 4
    load_coup.wait()
    ab = iota((1, R * R), 1)
    top = jnp.maximum(ab // R, ab % R)
    coup[...] = jnp.where(top < rank_c, coup[...].astype(F32), 0.0).astype(BF16)
    flip = ones_where(iota((R * R, 1), 0) == (ab % R) * R + ab // R)
    for i in range(4):
        part = pl.ds(i * 128, 128)
        coup_t[part, :] = dot(coup[part, :], flip).astype(BF16)

    own = iota((CL, CL * R), 1) // R == iota((CL, CL * R), 0)
    rows_of = ones_where(iota((ROWS, CL), 1) // 4 == iota((ROWS, CL), 0))
    even = iota((NEAR, 1), 0) % 2 == 0
    even_pair = iota((NEAR, 1), 0) % 4 < 2

    def four_blocks(k):
        first = near[pl.ds(k, 2)].reshape(2 * M, M)
        second = near[pl.ds(k + 2, 2)].reshape(2 * M, M)
        return jnp.concatenate([first, second], axis=1)

    pair_of_row = iota((16, 1), 0) // 2
    odd_row = iota((16, 1), 0) % 2 == 1

    field = rs_ref[...]
    residual = field
    solution = jnp.zeros_like(field)
    image = field

    for t in range(ITERS):
        low = field.astype(BF16)
        if t >= SHORT:
            sum_out[t - SHORT] = jnp.where(lane == 0, rw, jnp.where(lane == 1, ww, 0.0))
            sum_a[t - SHORT, 0] = sum_out[t - SHORT]
            for o in PLANE:
                pltpu.make_async_remote_copy(
                    sum_out.at[t - SHORT], sum_a.at[t - SHORT, o], tree_s.at[t - SHORT, 0], tree_r.at[t - SHORT, 0],
                    device_id=gx * 16 + (gy + o // 4) % 4 * 4 + (gz + o % 4) % 4, device_id_type=LOGICAL,
                ).start()
        win[t, 1] = low
        to_next = pltpu.make_async_remote_copy(
            win.at[t, 1], win.at[t, 0], wsem_s.at[t, 0], wsem_r.at[t, 0], device_id=nxt, device_id_type=LOGICAL
        )
        to_prev = pltpu.make_async_remote_copy(
            win.at[t, 1], win.at[t, 2], wsem_s.at[t, 1], wsem_r.at[t, 1], device_id=prv, device_id_type=LOGICAL
        )
        if t > 0:
            to_next.start()
            to_prev.start()

        raw = jnp.where(own, dot(low, basis_t[...]), 0.0)
        coeffs = (raw[:, 0:M] + raw[:, M : 2 * M] + raw[:, 2 * M : 3 * M] + raw[:, 3 * M : 4 * M]).astype(BF16)
        four = copies(coeffs.astype(F32))
        wide = dot(hrow[...], four.astype(BF16)).astype(BF16)
        if t == 0:
            for i in range(4):
                part = pl.ds(i * 128, 128)
                prods = coup_t[part, :].astype(F32) * jnp.concatenate([wide[i * 128 : (i + 1) * 128].astype(F32)] * 8, axis=1)
                hi, lo = split(prods)
                c4s[part, :] = ((dot(hi, e2_t[...]) + dot(lo, e2_t[...])) * jmask[part, :]).astype(BF16)
        else:
            prods = coup_t[...] * jnp.concatenate([wide] * 8, axis=1)
            c4s[...] = (dot(prods, e2_t[...]) * jmask[...]).astype(BF16)
        if t < SHORT:
            message = dot(t8[...], c4s[...])
            tile = dot(rows_of, coeffs)
            if t == 0:
                message = message + meta[...]
            send[t] = (message.reshape(N, ROWS, M) + tile[None]).astype(BF16)
            recv[t, N - 1] = send[t, me]
        else:
            spread4 = jnp.concatenate([jnp.where(lane // R == q, four, 0.0) for q in range(4)] + [jnp.zeros((64, M), F32)], axis=0)
            message = dot(t4[...], c4s[...]) + dot(pick4[...], spread4.astype(BF16))
            send4[t - SHORT] = message.reshape(N, 4, M).astype(BF16)
            recv4[t - SHORT, N - 1] = send4[t - SHORT, N - 1]

        def far_send(i, t=t):
            there = others[i]
            if t < SHORT:
                src, dst = send.at[t, there], recv.at[t, BACK[i]]
            else:
                src, dst = send4.at[t - SHORT, i], recv4.at[t - SHORT, BACK[i]]
            pltpu.make_async_remote_copy(
                src, dst, ssem.at[t], rsem.at[t], device_id=there, device_id_type=LOGICAL
            ).start()

        if t == 0:
            pl.semaphore_wait(barrier, N - 1)
            to_next.start()
            to_prev.start()
        for i in range(N - 1):
            far_send(i)
        if t == 0:
            gmask[...] = jnp.where(lane // R == local_c % 4, 1.0, 0.0)
            hrow_t[...] = ones_where(iota((CL, 1), 0) == frow)
            code_g = owner_c * ROWS + local_c // 4
            gx, gy, gz = lax.axis_index("gx"), lax.axis_index("gy"), lax.axis_index("gz")
            repeat4[...] = ones_where(iota((N * 4, N), 0) // 4 == iota((N * 4, N), 1))
            steps = table_ref[...]
            source = (
                (gx // 2 + steps[0:1]) % 4 * 32 + (gx % 2 + steps[1:2]) % 2 * 16 + (gy + steps[2:3]) % 4 * 4 + (gz + steps[3:4]) % 4
            )
            big[pl.ds(0, FAR), :] = ones_where(source[:, 0 : N * ROWS] * ROWS + iota((1, N * ROWS), 1) % ROWS == code_g)
            source4 = source[:, N * ROWS :]
            big4[pl.ds(0, FAR), :] = ones_where(source4 * 4 + iota((1, N * 4), 1) % 4 == owner_c * 4 + place_c // 4)
            source4_c = jnp.transpose(jnp.broadcast_to(source4.astype(F32), (8, N * 4)))[:, 0:1].astype(jnp.int32)
            t4[...] = ones_where(source4_c * 4 + row4 == owner * 4 + 2 + place // 4)
            count = ncount_ref[0, 0]
            live = iota((1, NEAR), 1) < count
            nrow = nrow_ref[...] - me * CL
            ncol = ncol_ref[...] - me * CL + CL
            hnr_t[...] = ones_where((iota((CL, 1), 0) == nrow) & live)
            hnc_t[...] = ones_where((iota((3 * CL, 1), 0) == ncol) & live)
            ncodes = jnp.concatenate([nrow.astype(F32), ncol.astype(F32), jnp.zeros((6, NEAR), F32)], axis=0)
            ncodes_t = jnp.transpose(ncodes)
            hnr[...] = ones_where(iota((1, CL), 1) == ncodes_t[:, 0:1].astype(jnp.int32))
            hnc[...] = ones_where(iota((1, 3 * CL), 1) == ncodes_t[:, 1:2].astype(jnp.int32))
        grow_t = dot(hnr[...], low)
        zero = jnp.zeros_like(grow_t)
        grow[...] = jnp.concatenate([jnp.where(even, grow_t, zero), jnp.where(even, zero, grow_t)], axis=1).astype(BF16)


        if t == 0:
            load_near.wait()

        def near_back(i, carry):
            part = pl.ds(i * 16, 16)
            lhs = grow[part, :]
            out = jnp.zeros((16, M), F32)
            for j in range(4):
                out_j = dot(lhs, four_blocks(i * 16 + 4 * j))
                out = jnp.where(pair_of_row == 2 * j, out_j[:, :M], out)
                out = jnp.where(pair_of_row == 2 * j + 1, out_j[:, M:], out)
            backs[part, :] = out
            return carry

        for i in range(12):
            near_back(i, 0)
        hi, lo = split(backs[...])
        spilled = dot(hnc_t[...], hi) + dot(hnc_t[...], lo)
        spout[t, 0] = spilled[0:CL]
        spout[t, 1] = spilled[2 * CL : 3 * CL]
        spill_prev = pltpu.make_async_remote_copy(
            spout.at[t, 0], spin.at[t, 1], psem_s.at[t, 0], psem_r.at[t, 1], device_id=prv, device_id_type=LOGICAL
        )
        spill_next = pltpu.make_async_remote_copy(
            spout.at[t, 1], spin.at[t, 0], psem_s.at[t, 1], psem_r.at[t, 0], device_id=nxt, device_id_type=LOGICAL
        )
        spill_prev.start()
        spill_next.start()
        if t >= SHORT:
            landed = sum_a.at[t - SHORT, pl.ds(1, 15)]
            pltpu.make_async_copy(landed, landed, tree_r.at[t - SHORT, 0]).wait()
            sum_mid[t - SHORT] = jnp.sum(sum_a[t - SHORT], axis=0)
            sum_b[t - SHORT, 0] = sum_mid[t - SHORT]
            for o in (4, 5, 2, 3, 6, 7, 1):
                pltpu.make_async_remote_copy(
                    sum_mid.at[t - SHORT], sum_b.at[t - SHORT, o], tree_s.at[t - SHORT, 1], tree_r.at[t - SHORT, 1],
                    device_id=(gx + o) % 8 * 16 + gy * 4 + gz, device_id_type=LOGICAL,
                ).start()

        to_next.wait_recv()
        to_prev.wait_recv()
        gath_t = dot(hnc[...], win[t].reshape(3 * CL, M))
        gath[...] = jnp.concatenate(
            [jnp.where(even_pair, gath_t, zero), jnp.where(even_pair, zero, gath_t)], axis=1
        ).astype(BF16)

        def near_forward(i, carry):
            part = pl.ds(i * 16, 16)
            lhs = gath[part, :]
            out = jnp.zeros((16, M), F32)
            for j in range(4):
                got = dot_t(lhs, four_blocks(i * 16 + 4 * j))
                got = jnp.where(odd_row, got[:, M:], got[:, :M])
                out = jnp.where(pair_of_row // 2 == j, got, out)
            fwds[part, :] = out
            return carry

        for i in range(12):
            near_forward(i, 0)
        hi, lo = split(fwds[...])
        product = diag_ref[...] * field + spilled[CL : 2 * CL] + dot(hnr_t[...], hi) + dot(hnr_t[...], lo)

        if t < SHORT:
            landed = recv.at[t, pl.ds(0, N - 1)]
            pltpu.make_async_copy(landed, landed, rsem.at[t]).wait()
            arrived = recv[t].reshape(N * ROWS, M)
            if t == 0:
                pick = ones_where(iota((16, M), 1) == iota((16, M), 0))
                numbers = dot_t(pick, arrived)
                col = iota((1, N * ROWS), 1) % ROWS
                first = jnp.concatenate([numbers[:, 3:], numbers[:, :3]], axis=1)
                second = jnp.concatenate([numbers[:, 2:], numbers[:, :2]], axis=1)
                pieces = []
                for q in range(4):
                    number = jnp.where(col == 4, first[q : q + 1], jnp.where(col == 5, second[4 + q : 5 + q], -1.0))
                    pieces.append(ones_where(iota((CL, 1), 0).astype(F32) == number))
                big[pl.ds(FAR, 64), :] = jnp.concatenate(pieces, axis=0)
            got = dot(big[...], arrived)
            numbers = dot(repeat4[...], recv[0].astype(F32)[:, 7, :].astype(BF16))
            numbers = jnp.where(row4 % 2 == 0, numbers, pltpu.roll(numbers, M - 4, 1))
            spread = ones_where((iota((M, M), 0) == iota((M, M), 1) // CL) & (iota((M, M), 0) < 4))
            numbers = dot(numbers.astype(BF16), spread)
            hot = jnp.where((iota((1, M), 1) % CL).astype(F32) == numbers, 1.0, 0.0)
            hot = jnp.where(iota((1, M), 1) < 64, hot, 0.0)
            pick4[...] = jnp.where(row4 < 2, hot, 0.0).astype(BF16)
            big4[pl.ds(FAR, 64), :] = jnp.transpose(jnp.where(row4 >= 2, hot, 0.0))[0:64, :].astype(BF16)
        else:
            landed = recv4.at[t - SHORT, pl.ds(0, N - 1)]
            pltpu.make_async_copy(landed, landed, rsem.at[t]).wait()
            got = dot(big4[...], recv4[t - SHORT].reshape(N * 4, M))
            landed = sum_b.at[t - SHORT, pl.ds(1, 7)]
            pltpu.make_async_copy(landed, landed, tree_r.at[t - SHORT, 1]).wait()
            totals = jnp.sum(sum_b[t - SHORT], axis=0)
            rw, ww = totals[:, 0:1], totals[:, 1:2]
        c4s[...] = copies(got[0:FAR] * (gmask if t < SHORT else jmask)[...]).astype(BF16)
        if t == 0:
            z = jnp.zeros((CL, R * R), F32)
            for i in range(4):
                part = pl.ds(i * 128, 128)
                c4 = c4s[part, :].astype(F32)
                hi, lo = split(coup[part, :].astype(F32) * jnp.concatenate([c4] * 8, axis=1))
                rows = hrow_t[:, i * 128 : (i + 1) * 128]
                z = z + dot(jnp.concatenate([rows, rows], axis=1), jnp.concatenate([hi, lo], axis=0))
        else:
            z = dot(hrow_t[...], coup[...] * jnp.concatenate([c4s[...]] * 8, axis=1))
        hi, lo = split(z)
        farsum = dot(jnp.concatenate([hi, lo], axis=0), e2_t[...])
        farsum = farsum[0:CL] + farsum[CL:]
        slots = jnp.zeros((CL, M), F32)
        for q in range(4):
            slots = slots + jnp.where(lane // R == q, got[FAR + 16 * q : FAR + 16 * (q + 1), :], 0.0)
        farsum = farsum + copies(slots)
        diag_far = jnp.where(own, jnp.concatenate([farsum] * 4, axis=1), 0.0).astype(BF16)
        product = product + dot(diag_far, basis_ref[...])

        spill_prev.wait_recv()
        spill_next.wait_recv()
        product = product + spin[t, 0] + spin[t, 1]

        if t == 0:
            image = product
        else:
            step = rw / (ww + EPS)
            solution = solution + step * residual
            residual = residual - step * image
            image = image - step * product
        field = image
        if t + 1 < ITERS:
            rw, ww = whole(residual * image), whole(image * image)

    rw, ww = whole(residual * image), whole(image * image)
    last_out[...] = jnp.where(lane == 0, rw, jnp.where(lane == 1, ww, 0.0))
    last_in[me] = last_out[...]

    for there in others:
        pltpu.make_async_remote_copy(
            last_out, last_in.at[me], lsem_s, lsem_r, device_id=there, device_id_type=LOGICAL
        ).start()
    for t in range(ITERS - SHORT):
        sent = sum_a.at[t, pl.ds(1, 15)]
        pltpu.make_async_copy(sent, sent, tree_s.at[t, 0]).wait()
        sent = sum_b.at[t, pl.ds(1, 7)]
        pltpu.make_async_copy(sent, sent, tree_s.at[t, 1]).wait()
    for t in range(ITERS):
        sent = send.at[t, pl.ds(0, N - 1)] if t < SHORT else send4.at[t - SHORT, pl.ds(0, N - 1)]
        pltpu.make_async_copy(sent, sent, ssem.at[t]).wait()
        for i in range(2):
            pltpu.make_async_copy(win.at[t, 1], win.at[t, 1], wsem_s.at[t, i]).wait()
            pltpu.make_async_copy(spout.at[t, i], spout.at[t, i], psem_s.at[t, i]).wait()
    everyone = last_in.at[pl.ds(0, N - 1)]
    pltpu.make_async_copy(everyone, everyone, lsem_r).wait()
    totals = jnp.sum(last_in[...], axis=0)
    step = totals[:, 0:1] / (totals[:, 1:2] + EPS)
    out_ref[0] = solution
    out_ref[1] = residual
    out_ref[2] = image
    out_ref[3] = jnp.broadcast_to(step, (CL, M))

    pltpu.make_async_copy(everyone, everyone, lsem_s).wait()


def on_device(rs, diag, near, nrow, ncol, ncount, basis, coup, frow, fcol, frank):
    vmem = pl.BlockSpec(memory_space=pltpu.VMEM)
    hbm = pl.BlockSpec(memory_space=pl.ANY)
    ints = jnp.int32
    v = pltpu.VMEM
    dma = pltpu.SemaphoreType.DMA
    out = pl.pallas_call(
        kernel,
        out_shape=jax.ShapeDtypeStruct((4, CL, M), F32),
        in_specs=[hbm] * 12,
        out_specs=vmem,
        scratch_shapes=[
            v((CL, M), F32),
            v((CL, M), F32),
            v((1, NEAR), ints),
            v((1, NEAR), ints),
            pltpu.SMEM((1, 1), ints),
            v((CL * R, M), BF16),
            v((1, FAR), ints),
            v((1, FAR), ints),
            v((1, FAR), ints),
            v((8, N * (ROWS + 4)), ints),
            v((NEAR, M, M), BF16),
            v((FAR, R * R), BF16),
            v((FAR, R * R), BF16),
            v((FAR + 64, N * ROWS), BF16),
            v((N * ROWS, FAR), BF16),
            v((R * R, M), BF16),
            v((M, CL * R), BF16),
            v((FAR, CL), BF16),
            v((CL, FAR), BF16),
            v((FAR, M), F32),
            v((FAR, M), F32),
            v((NEAR, CL), BF16),
            v((NEAR, 3 * CL), BF16),
            v((CL, NEAR), BF16),
            v((3 * CL, NEAR), BF16),
            v((N * ROWS, M), F32),
            v((FAR + 64, N * 4), BF16),
            v((N * 4, FAR), BF16),
            v((N * 4, M), BF16),
            v((N * 4, N), BF16),
            v((ITERS - SHORT, N, 4, M), BF16),
            v((ITERS - SHORT, N, 4, M), BF16),
            v((ITERS - SHORT, 1, M), F32),
            v((ITERS - SHORT, 16, 1, M), F32),
            v((ITERS - SHORT, 1, M), F32),
            v((ITERS - SHORT, 8, 1, M), F32),
            dma((ITERS - SHORT, 2)),
            dma((ITERS - SHORT, 2)),
            v((NEAR, 2 * M), BF16),
            v((NEAR, 2 * M), BF16),
            v((NEAR, M), F32),
            v((NEAR, M), F32),
            v((FAR, M), BF16),
            v((SHORT, N, ROWS, M), BF16),
            v((SHORT, N, ROWS, M), BF16),
            v((ITERS, 3, CL, M), BF16),
            v((ITERS, 2, CL, M), F32),
            v((ITERS, 2, CL, M), F32),
            v((1, M), F32),
            v((N, 1, M), F32),
            dma((12,)),
            dma((ITERS,)),
            dma((ITERS,)),
            dma((ITERS, 2)),
            dma((ITERS, 2)),
            dma((ITERS, 2)),
            dma((ITERS, 2)),
            dma,
            dma,
        ],
        compiler_params=pltpu.CompilerParams(
            collective_id=0, has_side_effects=True, vmem_limit_bytes=60 << 20
        ),
    )(
        rs,
        diag,
        near,
        nrow.reshape(1, NEAR),
        ncol.reshape(1, NEAR),
        ncount.reshape(1, 1),
        basis.reshape(CL * R, M),
        coup,
        frow.reshape(1, FAR),
        fcol.reshape(1, FAR),
        frank.reshape(1, FAR),
        jnp.asarray(order_table()),
    )
    return out[0] + out[3] * out[1], out[1] - out[3] * out[2]


def solution(mesh):
    flat = P(AXES)
    two = P(AXES, None)
    three = P(AXES, None, None)
    return jax.shard_map(
        on_device,
        mesh=mesh,
        in_specs=(two, two, three, flat, flat, flat, three, two, flat, flat, flat),
        out_specs=(two, two),
        check_vma=False,
    )
```

```python
import functools

import jax
import jax.numpy as jnp
import numpy as np
from jax import lax
from jax.experimental import pallas as pl
from jax.experimental.pallas import tpu as pltpu
from jax.sharding import PartitionSpec as P

ITERS = 3
AXES = ("gx", "gy", "gz")
N = 128
CL = 16
M = 128
R = 32
NEAR = 192
FAR = 512
ROWS = 8
EPS = 1e-6
F32, BF16 = jnp.float32, jnp.bfloat16
LOGICAL = pl.DeviceIdType.LOGICAL


STEPS = sorted(
    ((code, core) for code in range(64) for core in range(2) if (code, core) != (0, 0)),
    key=lambda s: (-bin(s[0]).count("1"), s[0], s[1]),
)
GRAY = (0, 1, 3, 2)
SHORT = 1
PLANE = sorted(range(1, 16), key=lambda o: -min(o // 4, 4 - o // 4) - min(o % 4, 4 - o % 4))
FIRST = 48
NEXT = 6
PLACE = {step: i for i, step in enumerate(STEPS)}
BACK = [
    PLACE[(sum((0, 2, 1, 3)[code >> shift & 3] << shift for shift in (0, 2, 4)), core)] for code, core in STEPS
]


def order_table():
    steps = STEPS + [(0, 0)]
    table = np.zeros((8, N * (ROWS + 4)), np.int32)
    for i, (code, core) in enumerate(steps):
        for part in (slice(i * ROWS, (i + 1) * ROWS), slice(N * ROWS + i * 4, N * ROWS + (i + 1) * 4)):
            table[0, part] = GRAY[code // 16]
            table[1, part] = core
            table[2, part] = GRAY[code // 4 % 4]
            table[3, part] = GRAY[code % 4]
    return table


def partners():
    gx, gy, gz = lax.axis_index("gx"), lax.axis_index("gy"), lax.axis_index("gz")
    x, core = gx // 2, gx % 2
    xs = [((x + step) % 4) * 32 for step in range(4)]
    cores = [core * 16, (1 - core) * 16]
    zs = [((gy + step) % 4) * 4 for step in range(4)]
    ys = [(gz + step) % 4 for step in range(4)]
    return [
        xs[GRAY[code // 16]] + cores[other] + zs[GRAY[code // 4 % 4]] + ys[GRAY[code % 4]] for code, other in STEPS
    ]


def iota(shape, dim):
    return lax.broadcasted_iota(jnp.int32, shape, dim)


def ones_where(cond):
    return jnp.where(cond, 1.0, 0.0).astype(BF16)


def dot(a, b):
    return jnp.dot(a, b, preferred_element_type=F32)


def dot_t(a, b):
    return lax.dot_general(a, b, (((1,), (1,)), ((), ())), preferred_element_type=F32)


def copies(x):
    x = x + pltpu.roll(x, 2 * R, 1)
    return x + pltpu.roll(x, R, 1)


def whole(x):
    return jnp.sum(jnp.sum(x, axis=0, keepdims=True), axis=1, keepdims=True)


def split(x):
    hi = x.astype(BF16)
    return hi, (x - hi.astype(F32)).astype(BF16)


def kernel(
    rs_hbm, diag_hbm, near_hbm, nrow_hbm, ncol_hbm, ncount_hbm, basis_hbm, coup_hbm, frow_hbm, fcol_hbm, frank_hbm, table_hbm,
    out_ref,
    rs_ref, diag_ref, nrow_ref, ncol_ref, ncount_ref, basis_ref, frow_ref, fcol_ref, frank_ref, table_ref,
    near, coup, coup_t, big, t8, e2_t, basis_t, hrow, hrow_t, gmask, jmask, hnr, hnc, hnr_t, hnc_t, meta,
    big4, t4, pick4, repeat4, send4, recv4, sum_out, sum_a, sum_mid, sum_b, tree_s, tree_r, gath, grow, backs, fwds, c4s, send, recv, win, spout, spin, last_out, last_in,
    dma_sem, ssem, rsem, wsem_s, wsem_r, psem_s, psem_r, lsem_s, lsem_r,
):
    me = lax.axis_index(AXES)
    nxt, prv = lax.rem(me + 1, N), lax.rem(me + N - 1, N)
    load_coup = pltpu.make_async_copy(coup_hbm, coup, dma_sem.at[0])
    load_near = pltpu.make_async_copy(near_hbm, near, dma_sem.at[1])
    pairs = (
        (frow_hbm, frow_ref), (fcol_hbm, fcol_ref), (frank_hbm, frank_ref), (nrow_hbm, nrow_ref), (ncol_hbm, ncol_ref),
        (ncount_hbm, ncount_ref), (rs_hbm, rs_ref), (basis_hbm, basis_ref), (diag_hbm, diag_ref), (table_hbm, table_ref),
    )
    loads = [pltpu.make_async_copy(a, b, dma_sem.at[2 + i]) for i, (a, b) in enumerate(pairs)]
    for load in loads:
        load.start()
    load_coup.start()
    load_near.start()

    barrier = pltpu.get_barrier_semaphore()

    others = partners()
    for there in others:
        pl.semaphore_signal(barrier, inc=1, device_id=there, device_id_type=LOGICAL)
    for load in loads:
        load.wait()

    frow = frow_ref[...] - me * CL
    fcol = fcol_ref[...]
    owner = fcol // CL
    local = fcol - owner * CL
    rank = frank_ref[...]
    owner_f = owner.astype(F32)
    codes = jnp.concatenate(
        [frow.astype(F32), owner_f, local.astype(F32), rank.astype(F32), jnp.zeros((4, FAR), F32)], axis=0
    )
    codes_t = jnp.transpose(codes)
    frow_c = codes_t[:, 0:1].astype(jnp.int32)
    owner_c = codes_t[:, 1:2].astype(jnp.int32)
    local_c = codes_t[:, 2:3].astype(jnp.int32)
    rank_c = codes_t[:, 3:4].astype(jnp.int32)
    same = jnp.where((owner_c == owner) & (iota((FAR, FAR), 0) < iota((FAR, FAR), 1)), 1.0, 0.0)
    place_f = jnp.sum(same, axis=0, keepdims=True)
    place = place_f.astype(jnp.int32)
    place_c = jnp.transpose(jnp.broadcast_to(place_f, (8, FAR)))[:, 0:1].astype(jnp.int32)

    lane = iota((1, M), 1)
    jmask[...] = jnp.where(lane // R == place_c % 4, 1.0, 0.0)
    hrow[...] = ones_where(iota((1, CL), 1) == frow_c)
    code_s = owner * ROWS + 4 + place // 4
    t8[...] = ones_where(iota((N * ROWS, 1), 0) == code_s)
    e2_t[...] = ones_where(iota((R * R, M), 0) // R == iota((R * R, M), 1) % R)
    eye = ones_where(iota((M, M), 0) == iota((M, M), 1))
    basis_t[...] = dot_t(eye, basis_ref[...]).astype(BF16)
    meta[...] = (jmask[...] * local_c.astype(F32)).astype(BF16)
    row4 = iota((N * 4, 1), 0) % 4
    load_coup.wait()
    ab = iota((1, R * R), 1)
    top = jnp.maximum(ab // R, ab % R)
    coup[...] = jnp.where(top < rank_c, coup[...].astype(F32), 0.0).astype(BF16)
    flip = ones_where(iota((R * R, 1), 0) == (ab % R) * R + ab // R)
    for i in range(4):
        part = pl.ds(i * 128, 128)
        coup_t[part, :] = dot(coup[part, :], flip).astype(BF16)

    own = iota((CL, CL * R), 1) // R == iota((CL, CL * R), 0)
    rows_of = ones_where(iota((ROWS, CL), 1) // 4 == iota((ROWS, CL), 0))
    even = iota((NEAR, 1), 0) % 2 == 0
    even_pair = iota((NEAR, 1), 0) % 4 < 2

    def four_blocks(k):
        first = near[pl.ds(k, 2)].reshape(2 * M, M)
        second = near[pl.ds(k + 2, 2)].reshape(2 * M, M)
        return jnp.concatenate([first, second], axis=1)

    pair_of_row = iota((16, 1), 0) // 2
    odd_row = iota((16, 1), 0) % 2 == 1

    field = rs_ref[...]
    residual = field
    solution = jnp.zeros_like(field)
    image = field

    for t in range(ITERS):
        low = field.astype(BF16)
        if t >= SHORT:
            sum_out[t - SHORT] = jnp.where(lane == 0, rw, jnp.where(lane == 1, ww, 0.0))
            sum_a[t - SHORT, 0] = sum_out[t - SHORT]
            for o in PLANE:
                pltpu.make_async_remote_copy(
                    sum_out.at[t - SHORT], sum_a.at[t - SHORT, o], tree_s.at[t - SHORT, 0], tree_r.at[t - SHORT, 0],
                    device_id=gx * 16 + (gy + o // 4) % 4 * 4 + (gz + o % 4) % 4, device_id_type=LOGICAL,
                ).start()
        win[t, 1] = low
        to_next = pltpu.make_async_remote_copy(
            win.at[t, 1], win.at[t, 0], wsem_s.at[t, 0], wsem_r.at[t, 0], device_id=nxt, device_id_type=LOGICAL
        )
        to_prev = pltpu.make_async_remote_copy(
            win.at[t, 1], win.at[t, 2], wsem_s.at[t, 1], wsem_r.at[t, 1], device_id=prv, device_id_type=LOGICAL
        )
        if t > 0:
            to_next.start()
            to_prev.start()

        raw = jnp.where(own, dot(low, basis_t[...]), 0.0)
        coeffs = (raw[:, 0:M] + raw[:, M : 2 * M] + raw[:, 2 * M : 3 * M] + raw[:, 3 * M : 4 * M]).astype(BF16)
        four = copies(coeffs.astype(F32))
        wide = dot(hrow[...], four.astype(BF16)).astype(BF16)
        if t == 0:
            for i in range(4):
                part = pl.ds(i * 128, 128)
                prods = coup_t[part, :].astype(F32) * jnp.concatenate([wide[i * 128 : (i + 1) * 128].astype(F32)] * 8, axis=1)
                hi, lo = split(prods)
                c4s[part, :] = ((dot(hi, e2_t[...]) + dot(lo, e2_t[...])) * jmask[part, :]).astype(BF16)
        else:
            prods = coup_t[...] * jnp.concatenate([wide] * 8, axis=1)
            c4s[...] = (dot(prods, e2_t[...]) * jmask[...]).astype(BF16)
        if t < SHORT:
            both = dot(t8[...], jnp.concatenate([c4s[...], meta[...]], axis=1))
            message = both[:, :M] + pltpu.roll(both[:, M:], 2, 0)
            tile = dot(rows_of, coeffs)
            send[t] = (message.reshape(N, ROWS, M) + tile[None]).astype(BF16)
            recv[t, N - 1] = send[t, me]
        else:
            spread4 = jnp.concatenate([jnp.where(lane // R == q, four, 0.0) for q in range(4)] + [jnp.zeros((64, M), F32)], axis=0)
            message = dot(t4[...], c4s[...]) + dot(pick4[...], spread4.astype(BF16))
            send4[t - SHORT] = message.reshape(N, 4, M).astype(BF16)
            recv4[t - SHORT, N - 1] = send4[t - SHORT, N - 1]

        def far_send(i, t=t):
            there = others[i]
            if t < SHORT:
                src, dst = send.at[t, there], recv.at[t, BACK[i]]
            else:
                src, dst = send4.at[t - SHORT, i], recv4.at[t - SHORT, BACK[i]]
            pltpu.make_async_remote_copy(
                src, dst, ssem.at[t], rsem.at[t], device_id=there, device_id_type=LOGICAL
            ).start()

        if t == 0:
            pl.semaphore_wait(barrier, N - 1)
            to_next.start()
            to_prev.start()
        for i in range(N - 1):
            far_send(i)
        if t == 0:
            gmask[...] = jnp.where(lane // R == local_c % 4, 1.0, 0.0)
            hrow_t[...] = ones_where(iota((CL, 1), 0) == frow)
            code_g = owner_c * ROWS + local_c // 4
            gx, gy, gz = lax.axis_index("gx"), lax.axis_index("gy"), lax.axis_index("gz")
            repeat4[...] = ones_where(iota((N * 4, 2 * N), 0) // 4 + iota((N * 4, 2 * N), 0) % 2 * N == iota((N * 4, 2 * N), 1))
            steps = table_ref[...]
            source = (
                (gx // 2 + steps[0:1]) % 4 * 32 + (gx % 2 + steps[1:2]) % 2 * 16 + (gy + steps[2:3]) % 4 * 4 + (gz + steps[3:4]) % 4
            )
            big[pl.ds(0, FAR), :] = ones_where(source[:, 0 : N * ROWS] * ROWS + iota((1, N * ROWS), 1) % ROWS == code_g)
            source4 = source[:, N * ROWS :]
            big4[pl.ds(0, FAR), :] = ones_where(source4 * 4 + iota((1, N * 4), 1) % 4 == owner_c * 4 + place_c // 4)
            source4_c = jnp.transpose(jnp.broadcast_to(source4.astype(F32), (8, N * 4)))[:, 0:1].astype(jnp.int32)
            t4[...] = ones_where(source4_c * 4 + row4 == owner * 4 + 2 + place // 4)
            count = ncount_ref[0, 0]
            live = iota((1, NEAR), 1) < count
            nrow = nrow_ref[...] - me * CL
            ncol = ncol_ref[...] - me * CL + CL
            hnr_t[...] = ones_where((iota((CL, 1), 0) == nrow) & live)
            hnc_t[...] = ones_where((iota((3 * CL, 1), 0) == ncol) & live)
            ncodes = jnp.concatenate([nrow.astype(F32), ncol.astype(F32), jnp.zeros((6, NEAR), F32)], axis=0)
            ncodes_t = jnp.transpose(ncodes)
            hnr[...] = ones_where(iota((1, CL), 1) == ncodes_t[:, 0:1].astype(jnp.int32))
            hnc[...] = ones_where(iota((1, 3 * CL), 1) == ncodes_t[:, 1:2].astype(jnp.int32))
        grow_t = dot(hnr[...], low)
        zero = jnp.zeros_like(grow_t)
        grow[...] = jnp.concatenate([jnp.where(even, grow_t, zero), jnp.where(even, zero, grow_t)], axis=1).astype(BF16)


        if t == 0:
            load_near.wait()

        def near_back(i, carry):
            part = pl.ds(i * 16, 16)
            lhs = grow[part, :]
            out = jnp.zeros((16, M), F32)
            for j in range(4):
                out_j = dot(lhs, four_blocks(i * 16 + 4 * j))
                out = jnp.where(pair_of_row == 2 * j, out_j[:, :M], out)
                out = jnp.where(pair_of_row == 2 * j + 1, out_j[:, M:], out)
            backs[part, :] = out
            return carry

        for i in range(12):
            near_back(i, 0)
        hi, lo = split(backs[...])
        spilled = dot(hnc_t[...], hi) + dot(hnc_t[...], lo)
        spout[t, 0] = spilled[0:CL]
        spout[t, 1] = spilled[2 * CL : 3 * CL]
        spill_prev = pltpu.make_async_remote_copy(
            spout.at[t, 0], spin.at[t, 1], psem_s.at[t, 0], psem_r.at[t, 1], device_id=prv, device_id_type=LOGICAL
        )
        spill_next = pltpu.make_async_remote_copy(
            spout.at[t, 1], spin.at[t, 0], psem_s.at[t, 1], psem_r.at[t, 0], device_id=nxt, device_id_type=LOGICAL
        )
        spill_prev.start()
        spill_next.start()
        if t >= SHORT:
            landed = sum_a.at[t - SHORT, pl.ds(1, 15)]
            pltpu.make_async_copy(landed, landed, tree_r.at[t - SHORT, 0]).wait()
            sum_mid[t - SHORT] = jnp.sum(sum_a[t - SHORT], axis=0)
            sum_b[t - SHORT, 0] = sum_mid[t - SHORT]
            for o in (4, 5, 2, 3, 6, 7, 1):
                pltpu.make_async_remote_copy(
                    sum_mid.at[t - SHORT], sum_b.at[t - SHORT, o], tree_s.at[t - SHORT, 1], tree_r.at[t - SHORT, 1],
                    device_id=(gx + o) % 8 * 16 + gy * 4 + gz, device_id_type=LOGICAL,
                ).start()

        to_next.wait_recv()
        to_prev.wait_recv()
        gath_t = dot(hnc[...], win[t].reshape(3 * CL, M))
        gath[...] = jnp.concatenate(
            [jnp.where(even_pair, gath_t, zero), jnp.where(even_pair, zero, gath_t)], axis=1
        ).astype(BF16)

        def near_forward(i, carry):
            part = pl.ds(i * 16, 16)
            lhs = gath[part, :]
            out = jnp.zeros((16, M), F32)
            for j in range(4):
                got = dot_t(lhs, four_blocks(i * 16 + 4 * j))
                got = jnp.where(odd_row, got[:, M:], got[:, :M])
                out = jnp.where(pair_of_row // 2 == j, got, out)
            fwds[part, :] = out
            return carry

        for i in range(12):
            near_forward(i, 0)
        hi, lo = split(fwds[...])
        product = diag_ref[...] * field + spilled[CL : 2 * CL] + dot(hnr_t[...], hi) + dot(hnr_t[...], lo)

        if t < SHORT:
            landed = recv.at[t, pl.ds(0, N - 1)]
            pltpu.make_async_copy(landed, landed, rsem.at[t]).wait()
            arrived = recv[t].reshape(N * ROWS, M)
            if t == 0:
                pick = ones_where(iota((16, M), 1) == iota((16, M), 0) * R)
                numbers = dot_t(pick, arrived)
                col = iota((1, N * ROWS), 1) % ROWS
                numbers = jnp.concatenate([numbers[:, 2:], numbers[:, :2]], axis=1)
                pieces = []
                for q in range(4):
                    number = jnp.where((col == 4) | (col == 5), numbers[q : q + 1], -1.0)
                    pieces.append(ones_where(iota((CL, 1), 0).astype(F32) == number))
                big[pl.ds(FAR, 64), :] = jnp.concatenate(pieces, axis=0)
            got = dot(big[...], arrived)
            rows = recv[0].astype(F32)
            rows = jnp.concatenate([rows[:, 6, :], rows[:, 7, :]], axis=0).astype(BF16)
            numbers = dot(repeat4[...], rows)
            spread = ones_where(iota((M, M), 0) == iota((M, M), 1) // CL * R)
            numbers = dot(numbers.astype(BF16), spread)
            hot = jnp.where((iota((1, M), 1) % CL).astype(F32) == numbers, 1.0, 0.0)
            hot = jnp.where(iota((1, M), 1) < 64, hot, 0.0)
            pick4[...] = jnp.where(row4 < 2, hot, 0.0).astype(BF16)
            big4[pl.ds(FAR, 64), :] = jnp.transpose(jnp.where(row4 >= 2, hot, 0.0))[0:64, :].astype(BF16)
        else:
            landed = recv4.at[t - SHORT, pl.ds(0, N - 1)]
            pltpu.make_async_copy(landed, landed, rsem.at[t]).wait()
            got = dot(big4[...], recv4[t - SHORT].reshape(N * 4, M))
            landed = sum_b.at[t - SHORT, pl.ds(1, 7)]
            pltpu.make_async_copy(landed, landed, tree_r.at[t - SHORT, 1]).wait()
            totals = jnp.sum(sum_b[t - SHORT], axis=0)
            rw, ww = totals[:, 0:1], totals[:, 1:2]
        c4s[...] = copies(got[0:FAR] * (gmask if t < SHORT else jmask)[...]).astype(BF16)
        if t == 0:
            z = jnp.zeros((CL, R * R), F32)
            for i in range(4):
                part = pl.ds(i * 128, 128)
                c4 = c4s[part, :].astype(F32)
                hi, lo = split(coup[part, :].astype(F32) * jnp.concatenate([c4] * 8, axis=1))
                rows = hrow_t[:, i * 128 : (i + 1) * 128]
                z = z + dot(jnp.concatenate([rows, rows], axis=1), jnp.concatenate([hi, lo], axis=0))
        else:
            z = dot(hrow_t[...], coup[...] * jnp.concatenate([c4s[...]] * 8, axis=1))
        hi, lo = split(z)
        farsum = dot(jnp.concatenate([hi, lo], axis=0), e2_t[...])
        farsum = farsum[0:CL] + farsum[CL:]
        slots = jnp.zeros((CL, M), F32)
        for q in range(4):
            slots = slots + jnp.where(lane // R == q, got[FAR + 16 * q : FAR + 16 * (q + 1), :], 0.0)
        farsum = farsum + copies(slots)
        diag_far = jnp.where(own, jnp.concatenate([farsum] * 4, axis=1), 0.0).astype(BF16)
        product = product + dot(diag_far, basis_ref[...])

        spill_prev.wait_recv()
        spill_next.wait_recv()
        product = product + spin[t, 0] + spin[t, 1]

        if t == 0:
            image = product
        else:
            step = rw / (ww + EPS)
            solution = solution + step * residual
            residual = residual - step * image
            image = image - step * product
        field = image
        if t + 1 < ITERS:
            rw, ww = whole(residual * image), whole(image * image)

    rw, ww = whole(residual * image), whole(image * image)
    last_out[...] = jnp.where(lane == 0, rw, jnp.where(lane == 1, ww, 0.0))
    last_in[me] = last_out[...]

    for there in others:
        pltpu.make_async_remote_copy(
            last_out, last_in.at[me], lsem_s, lsem_r, device_id=there, device_id_type=LOGICAL
        ).start()
    for t in range(ITERS - SHORT):
        sent = sum_a.at[t, pl.ds(1, 15)]
        pltpu.make_async_copy(sent, sent, tree_s.at[t, 0]).wait()
        sent = sum_b.at[t, pl.ds(1, 7)]
        pltpu.make_async_copy(sent, sent, tree_s.at[t, 1]).wait()
    for t in range(ITERS):
        sent = send.at[t, pl.ds(0, N - 1)] if t < SHORT else send4.at[t - SHORT, pl.ds(0, N - 1)]
        pltpu.make_async_copy(sent, sent, ssem.at[t]).wait()
        for i in range(2):
            pltpu.make_async_copy(win.at[t, 1], win.at[t, 1], wsem_s.at[t, i]).wait()
            pltpu.make_async_copy(spout.at[t, i], spout.at[t, i], psem_s.at[t, i]).wait()
    everyone = last_in.at[pl.ds(0, N - 1)]
    pltpu.make_async_copy(everyone, everyone, lsem_r).wait()
    totals = jnp.sum(last_in[...], axis=0)
    step = totals[:, 0:1] / (totals[:, 1:2] + EPS)
    out_ref[0] = solution
    out_ref[1] = residual
    out_ref[2] = image
    out_ref[3] = jnp.broadcast_to(step, (CL, M))

    pltpu.make_async_copy(everyone, everyone, lsem_s).wait()


def on_device(rs, diag, near, nrow, ncol, ncount, basis, coup, frow, fcol, frank):
    vmem = pl.BlockSpec(memory_space=pltpu.VMEM)
    hbm = pl.BlockSpec(memory_space=pl.ANY)
    ints = jnp.int32
    v = pltpu.VMEM
    dma = pltpu.SemaphoreType.DMA
    out = pl.pallas_call(
        kernel,
        out_shape=jax.ShapeDtypeStruct((4, CL, M), F32),
        in_specs=[hbm] * 12,
        out_specs=vmem,
        scratch_shapes=[
            v((CL, M), F32),
            v((CL, M), F32),
            v((1, NEAR), ints),
            v((1, NEAR), ints),
            pltpu.SMEM((1, 1), ints),
            v((CL * R, M), BF16),
            v((1, FAR), ints),
            v((1, FAR), ints),
            v((1, FAR), ints),
            v((8, N * (ROWS + 4)), ints),
            v((NEAR, M, M), BF16),
            v((FAR, R * R), BF16),
            v((FAR, R * R), BF16),
            v((FAR + 64, N * ROWS), BF16),
            v((N * ROWS, FAR), BF16),
            v((R * R, M), BF16),
            v((M, CL * R), BF16),
            v((FAR, CL), BF16),
            v((CL, FAR), BF16),
            v((FAR, M), F32),
            v((FAR, M), F32),
            v((NEAR, CL), BF16),
            v((NEAR, 3 * CL), BF16),
            v((CL, NEAR), BF16),
            v((3 * CL, NEAR), BF16),
            v((FAR, M), BF16),
            v((FAR + 64, N * 4), BF16),
            v((N * 4, FAR), BF16),
            v((N * 4, M), BF16),
            v((N * 4, 2 * N), BF16),
            v((ITERS - SHORT, N, 4, M), BF16),
            v((ITERS - SHORT, N, 4, M), BF16),
            v((ITERS - SHORT, 1, M), F32),
            v((ITERS - SHORT, 16, 1, M), F32),
            v((ITERS - SHORT, 1, M), F32),
            v((ITERS - SHORT, 8, 1, M), F32),
            dma((ITERS - SHORT, 2)),
            dma((ITERS - SHORT, 2)),
            v((NEAR, 2 * M), BF16),
            v((NEAR, 2 * M), BF16),
            v((NEAR, M), F32),
            v((NEAR, M), F32),
            v((FAR, M), BF16),
            v((SHORT, N, ROWS, M), BF16),
            v((SHORT, N, ROWS, M), BF16),
            v((ITERS, 3, CL, M), BF16),
            v((ITERS, 2, CL, M), F32),
            v((ITERS, 2, CL, M), F32),
            v((1, M), F32),
            v((N, 1, M), F32),
            dma((12,)),
            dma((ITERS,)),
            dma((ITERS,)),
            dma((ITERS, 2)),
            dma((ITERS, 2)),
            dma((ITERS, 2)),
            dma((ITERS, 2)),
            dma,
            dma,
        ],
        compiler_params=pltpu.CompilerParams(
            collective_id=0, has_side_effects=True, vmem_limit_bytes=60 << 20
        ),
    )(
        rs,
        diag,
        near,
        nrow.reshape(1, NEAR),
        ncol.reshape(1, NEAR),
        ncount.reshape(1, 1),
        basis.reshape(CL * R, M),
        coup,
        frow.reshape(1, FAR),
        fcol.reshape(1, FAR),
        frank.reshape(1, FAR),
        jnp.asarray(order_table()),
    )
    return out[0] + out[3] * out[1], out[1] - out[3] * out[2]


def solution(mesh):
    flat = P(AXES)
    two = P(AXES, None)
    three = P(AXES, None, None)
    return jax.shard_map(
        on_device,
        mesh=mesh,
        in_specs=(two, two, three, flat, flat, flat, three, two, flat, flat, flat),
        out_specs=(two, two),
        check_vma=False,
    )
```

```python
import functools

import jax
import jax.numpy as jnp
import numpy as np
from jax import lax
from jax.experimental import pallas as pl
from jax.experimental.pallas import tpu as pltpu
from jax.sharding import PartitionSpec as P

ITERS = 3
AXES = ("gx", "gy", "gz")
N = 128
CL = 16
M = 128
R = 32
NEAR = 192
FAR = 512
ROWS = 8
EPS = 1e-6
F32, BF16 = jnp.float32, jnp.bfloat16
LOGICAL = pl.DeviceIdType.LOGICAL


STEPS = sorted(
    ((code, core) for code in range(64) for core in range(2) if (code, core) != (0, 0)),
    key=lambda s: (-bin(s[0]).count("1"), s[0], s[1]),
)
GRAY = (0, 1, 3, 2)
SHORT = 1
PLANE = sorted(range(1, 16), key=lambda o: -min(o // 4, 4 - o // 4) - min(o % 4, 4 - o % 4))
FIRST = 48
NEXT = 6
PLACE = {step: i for i, step in enumerate(STEPS)}
BACK = [
    PLACE[(sum((0, 2, 1, 3)[code >> shift & 3] << shift for shift in (0, 2, 4)), core)] for code, core in STEPS
]


def order_table():
    steps = STEPS + [(0, 0)]
    table = np.zeros((8, N * (ROWS + 4)), np.int32)
    for i, (code, core) in enumerate(steps):
        for part in (slice(i * ROWS, (i + 1) * ROWS), slice(N * ROWS + i * 4, N * ROWS + (i + 1) * 4)):
            table[0, part] = GRAY[code // 16]
            table[1, part] = core
            table[2, part] = GRAY[code // 4 % 4]
            table[3, part] = GRAY[code % 4]
    return table


def partners():
    gx, gy, gz = lax.axis_index("gx"), lax.axis_index("gy"), lax.axis_index("gz")
    x, core = gx // 2, gx % 2
    xs = [((x + step) % 4) * 32 for step in range(4)]
    cores = [core * 16, (1 - core) * 16]
    zs = [((gy + step) % 4) * 4 for step in range(4)]
    ys = [(gz + step) % 4 for step in range(4)]
    return [
        xs[GRAY[code // 16]] + cores[other] + zs[GRAY[code // 4 % 4]] + ys[GRAY[code % 4]] for code, other in STEPS
    ]


def iota(shape, dim):
    return lax.broadcasted_iota(jnp.int32, shape, dim)


def ones_where(cond):
    return jnp.where(cond, 1.0, 0.0).astype(BF16)


def dot(a, b):
    return jnp.dot(a, b, preferred_element_type=F32)


def dot_t(a, b):
    return lax.dot_general(a, b, (((1,), (1,)), ((), ())), preferred_element_type=F32)


def copies(x):
    x = x + pltpu.roll(x, 2 * R, 1)
    return x + pltpu.roll(x, R, 1)


def whole(x):
    return jnp.sum(jnp.sum(x, axis=0, keepdims=True), axis=1, keepdims=True)


def split(x):
    hi = x.astype(BF16)
    return hi, (x - hi.astype(F32)).astype(BF16)


def kernel(
    rs_hbm, diag_hbm, near_hbm, nrow_hbm, ncol_hbm, ncount_hbm, basis_hbm, coup_hbm, frow_hbm, fcol_hbm, frank_hbm, table_hbm,
    out_ref,
    rs_ref, diag_ref, nrow_ref, ncol_ref, ncount_ref, basis_ref, frow_ref, fcol_ref, frank_ref, table_ref,
    near, coup, coup_t, big, t8, e2_t, basis_t, hrow, hrow_t, gmask, jmask, hnr, hnc, hnr_t, hnc_t, meta,
    big4, t4, pick4, repeat4, send4, recv4, sum_out, sum_a, sum_mid, sum_b, tree_s, tree_r, gath, grow, backs, fwds, c4s, send, recv, win, spout, spin, last_out, last_in,
    dma_sem, ssem, rsem, wsem_s, wsem_r, psem_s, psem_r, lsem_s, lsem_r,
):
    me = lax.axis_index(AXES)
    nxt, prv = lax.rem(me + 1, N), lax.rem(me + N - 1, N)
    load_coup = pltpu.make_async_copy(coup_hbm, coup, dma_sem.at[0])
    load_near = pltpu.make_async_copy(near_hbm, near, dma_sem.at[1])
    pairs = (
        (frow_hbm, frow_ref), (fcol_hbm, fcol_ref), (frank_hbm, frank_ref), (nrow_hbm, nrow_ref), (ncol_hbm, ncol_ref),
        (ncount_hbm, ncount_ref), (rs_hbm, rs_ref), (basis_hbm, basis_ref), (diag_hbm, diag_ref), (table_hbm, table_ref),
    )
    loads = [pltpu.make_async_copy(a, b, dma_sem.at[2 + i]) for i, (a, b) in enumerate(pairs)]
    for load in loads:
        load.start()
    load_coup.start()
    load_near.start()

    barrier = pltpu.get_barrier_semaphore()

    others = partners()
    for there in others:
        pl.semaphore_signal(barrier, inc=1, device_id=there, device_id_type=LOGICAL)
    for load in loads:
        load.wait()

    frow = frow_ref[...] - me * CL
    fcol = fcol_ref[...]
    owner = fcol // CL
    local = fcol - owner * CL
    rank = frank_ref[...]
    owner_f = owner.astype(F32)
    codes = jnp.concatenate(
        [frow.astype(F32), owner_f, local.astype(F32), rank.astype(F32), jnp.zeros((4, FAR), F32)], axis=0
    )
    codes_t = jnp.transpose(codes)
    frow_c = codes_t[:, 0:1].astype(jnp.int32)
    owner_c = codes_t[:, 1:2].astype(jnp.int32)
    local_c = codes_t[:, 2:3].astype(jnp.int32)
    rank_c = codes_t[:, 3:4].astype(jnp.int32)
    same = jnp.where((owner_c == owner) & (iota((FAR, FAR), 0) < iota((FAR, FAR), 1)), 1.0, 0.0)
    place_f = jnp.sum(same, axis=0, keepdims=True)
    place = place_f.astype(jnp.int32)
    place_c = jnp.transpose(jnp.broadcast_to(place_f, (8, FAR)))[:, 0:1].astype(jnp.int32)

    lane = iota((1, M), 1)
    jmask[...] = jnp.where(lane // R == place_c % 4, 1.0, 0.0)
    hrow[...] = ones_where(iota((1, CL), 1) == frow_c)
    code_s = owner * ROWS + 4 + place // 4
    t8[...] = ones_where(iota((N * ROWS, 1), 0) == code_s)
    e2_t[...] = ones_where(iota((R * R, M), 0) // R == iota((R * R, M), 1) % R)
    eye = ones_where(iota((M, M), 0) == iota((M, M), 1))
    basis_t[...] = dot_t(eye, basis_ref[...]).astype(BF16)
    meta[...] = (jmask[...] * local_c.astype(F32)).astype(BF16)
    row4 = iota((N * 4, 1), 0) % 4
    load_coup.wait()
    ab = iota((1, R * R), 1)
    top = jnp.maximum(ab // R, ab % R)
    coup[...] = jnp.where(top < rank_c, coup[...].astype(F32), 0.0).astype(BF16)
    flip = ones_where(iota((R * R, 1), 0) == (ab % R) * R + ab // R)
    for i in range(4):
        part = pl.ds(i * 128, 128)
        coup_t[part, :] = dot(coup[part, :], flip).astype(BF16)

    own = iota((CL, CL * R), 1) // R == iota((CL, CL * R), 0)
    rows_of = ones_where(iota((ROWS, CL), 1) // 4 == iota((ROWS, CL), 0))
    even = iota((NEAR, 1), 0) % 2 == 0
    even_pair = iota((NEAR, 1), 0) % 4 < 2

    def four_blocks(k):
        first = near[pl.ds(k, 2)].reshape(2 * M, M)
        second = near[pl.ds(k + 2, 2)].reshape(2 * M, M)
        return jnp.concatenate([first, second], axis=1)

    pair_of_row = iota((16, 1), 0) // 2
    odd_row = iota((16, 1), 0) % 2 == 1

    field = rs_ref[...]
    residual = field
    solution = jnp.zeros_like(field)
    image = field

    for t in range(ITERS):
        low = field.astype(BF16)
        if t >= SHORT:
            sum_out[t - SHORT] = jnp.where(lane == 0, rw, jnp.where(lane == 1, ww, 0.0))
            sum_a[t - SHORT, 0] = sum_out[t - SHORT]
            for o in PLANE:
                pltpu.make_async_remote_copy(
                    sum_out.at[t - SHORT], sum_a.at[t - SHORT, o], tree_s.at[t - SHORT, 0], tree_r.at[t - SHORT, 0],
                    device_id=gx * 16 + (gy + o // 4) % 4 * 4 + (gz + o % 4) % 4, device_id_type=LOGICAL,
                ).start()
        win[t, 1] = low
        to_next = pltpu.make_async_remote_copy(
            win.at[t, 1], win.at[t, 0], wsem_s.at[t, 0], wsem_r.at[t, 0], device_id=nxt, device_id_type=LOGICAL
        )
        to_prev = pltpu.make_async_remote_copy(
            win.at[t, 1], win.at[t, 2], wsem_s.at[t, 1], wsem_r.at[t, 1], device_id=prv, device_id_type=LOGICAL
        )
        if t > 0:
            to_next.start()
            to_prev.start()

        raw = jnp.where(own, dot(low, basis_t[...]), 0.0)
        coeffs = (raw[:, 0:M] + raw[:, M : 2 * M] + raw[:, 2 * M : 3 * M] + raw[:, 3 * M : 4 * M]).astype(BF16)
        four = copies(coeffs.astype(F32))
        wide = dot(hrow[...], four.astype(BF16)).astype(BF16)
        if t == 0:
            for i in range(4):
                part = pl.ds(i * 128, 128)
                prods = coup_t[part, :].astype(F32) * jnp.concatenate([wide[i * 128 : (i + 1) * 128].astype(F32)] * 8, axis=1)
                hi, lo = split(prods)
                pair = dot(jnp.concatenate([hi, lo], axis=0), e2_t[...])
                c4s[part, :] = ((pair[:128] + pair[128:]) * jmask[part, :]).astype(BF16)
        else:
            prods = coup_t[...] * jnp.concatenate([wide] * 8, axis=1)
            c4s[...] = (dot(prods, e2_t[...]) * jmask[...]).astype(BF16)
        if t < SHORT:
            both = dot(t8[...], jnp.concatenate([c4s[...], meta[...]], axis=1))
            message = both[:, :M] + pltpu.roll(both[:, M:], 2, 0)
            tile = dot(rows_of, coeffs)
            send[t] = (message.reshape(N, ROWS, M) + tile[None]).astype(BF16)
            recv[t, N - 1] = send[t, me]
        else:
            spread4 = jnp.concatenate([jnp.where(lane // R == q, four, 0.0) for q in range(4)] + [jnp.zeros((64, M), F32)], axis=0)
            message = dot(t4[...], c4s[...]) + dot(pick4[...], spread4.astype(BF16))
            send4[t - SHORT] = message.reshape(N, 4, M).astype(BF16)
            recv4[t - SHORT, N - 1] = send4[t - SHORT, N - 1]

        def far_send(i, t=t):
            there = others[i]
            if t < SHORT:
                src, dst = send.at[t, there], recv.at[t, BACK[i]]
            else:
                src, dst = send4.at[t - SHORT, i], recv4.at[t - SHORT, BACK[i]]
            pltpu.make_async_remote_copy(
                src, dst, ssem.at[t], rsem.at[t], device_id=there, device_id_type=LOGICAL
            ).start()

        if t == 0:
            pl.semaphore_wait(barrier, N - 1)
            to_next.start()
            to_prev.start()
        for i in range(N - 1):
            far_send(i)
        if t == 0:
            gmask[...] = jnp.where(lane // R == local_c % 4, 1.0, 0.0)
            hrow_t[...] = ones_where(iota((CL, 1), 0) == frow)
            code_g = owner_c * ROWS + local_c // 4
            gx, gy, gz = lax.axis_index("gx"), lax.axis_index("gy"), lax.axis_index("gz")
            repeat4[...] = ones_where(iota((N * 4, 2 * N), 0) // 4 + iota((N * 4, 2 * N), 0) % 2 * N == iota((N * 4, 2 * N), 1))
            steps = table_ref[...]
            source = (
                (gx // 2 + steps[0:1]) % 4 * 32 + (gx % 2 + steps[1:2]) % 2 * 16 + (gy + steps[2:3]) % 4 * 4 + (gz + steps[3:4]) % 4
            )
            big[pl.ds(0, FAR), :] = ones_where(source[:, 0 : N * ROWS] * ROWS + iota((1, N * ROWS), 1) % ROWS == code_g)
            source4 = source[:, N * ROWS :]
            big4[pl.ds(0, FAR), :] = ones_where(source4 * 4 + iota((1, N * 4), 1) % 4 == owner_c * 4 + place_c // 4)
            source4_c = jnp.transpose(jnp.broadcast_to(source4.astype(F32), (8, N * 4)))[:, 0:1].astype(jnp.int32)
            t4[...] = ones_where(source4_c * 4 + row4 == owner * 4 + 2 + place // 4)
            count = ncount_ref[0, 0]
            live = iota((1, NEAR), 1) < count
            nrow = nrow_ref[...] - me * CL
            ncol = ncol_ref[...] - me * CL + CL
            hnr_t[...] = ones_where((iota((CL, 1), 0) == nrow) & live)
            hnc_t[...] = ones_where((iota((3 * CL, 1), 0) == ncol) & live)
            ncodes = jnp.concatenate([nrow.astype(F32), ncol.astype(F32), jnp.zeros((6, NEAR), F32)], axis=0)
            ncodes_t = jnp.transpose(ncodes)
            hnr[...] = ones_where(iota((1, CL), 1) == ncodes_t[:, 0:1].astype(jnp.int32))
            hnc[...] = ones_where(iota((1, 3 * CL), 1) == ncodes_t[:, 1:2].astype(jnp.int32))
        grow_t = dot(hnr[...], low)
        zero = jnp.zeros_like(grow_t)
        grow[...] = jnp.concatenate([jnp.where(even, grow_t, zero), jnp.where(even, zero, grow_t)], axis=1).astype(BF16)


        if t == 0:
            load_near.wait()

        def near_back(i, carry):
            part = pl.ds(i * 16, 16)
            lhs = grow[part, :]
            out = jnp.zeros((16, M), F32)
            for j in range(4):
                out_j = dot(lhs, four_blocks(i * 16 + 4 * j))
                out = jnp.where(pair_of_row == 2 * j, out_j[:, :M], out)
                out = jnp.where(pair_of_row == 2 * j + 1, out_j[:, M:], out)
            backs[part, :] = out
            return carry

        for i in range(12):
            near_back(i, 0)
        hi, lo = split(backs[...])
        spilled = dot(hnc_t[...], hi) + dot(hnc_t[...], lo)
        spout[t, 0] = spilled[0:CL]
        spout[t, 1] = spilled[2 * CL : 3 * CL]
        spill_prev = pltpu.make_async_remote_copy(
            spout.at[t, 0], spin.at[t, 1], psem_s.at[t, 0], psem_r.at[t, 1], device_id=prv, device_id_type=LOGICAL
        )
        spill_next = pltpu.make_async_remote_copy(
            spout.at[t, 1], spin.at[t, 0], psem_s.at[t, 1], psem_r.at[t, 0], device_id=nxt, device_id_type=LOGICAL
        )
        spill_prev.start()
        spill_next.start()
        if t >= SHORT:
            landed = sum_a.at[t - SHORT, pl.ds(1, 15)]
            pltpu.make_async_copy(landed, landed, tree_r.at[t - SHORT, 0]).wait()
            sum_mid[t - SHORT] = jnp.sum(sum_a[t - SHORT], axis=0)
            sum_b[t - SHORT, 0] = sum_mid[t - SHORT]
            for o in (4, 5, 2, 3, 6, 7, 1):
                pltpu.make_async_remote_copy(
                    sum_mid.at[t - SHORT], sum_b.at[t - SHORT, o], tree_s.at[t - SHORT, 1], tree_r.at[t - SHORT, 1],
                    device_id=(gx + o) % 8 * 16 + gy * 4 + gz, device_id_type=LOGICAL,
                ).start()

        to_next.wait_recv()
        to_prev.wait_recv()
        gath_t = dot(hnc[...], win[t].reshape(3 * CL, M))
        gath[...] = jnp.concatenate(
            [jnp.where(even_pair, gath_t, zero), jnp.where(even_pair, zero, gath_t)], axis=1
        ).astype(BF16)

        def near_forward(i, carry):
            part = pl.ds(i * 16, 16)
            lhs = gath[part, :]
            out = jnp.zeros((16, M), F32)
            for j in range(4):
                got = dot_t(lhs, four_blocks(i * 16 + 4 * j))
                got = jnp.where(odd_row, got[:, M:], got[:, :M])
                out = jnp.where(pair_of_row // 2 == j, got, out)
            fwds[part, :] = out
            return carry

        for i in range(12):
            near_forward(i, 0)
        hi, lo = split(fwds[...])
        product = diag_ref[...] * field + spilled[CL : 2 * CL] + dot(hnr_t[...], hi) + dot(hnr_t[...], lo)

        if t < SHORT:
            landed = recv.at[t, pl.ds(0, N - 1)]
            pltpu.make_async_copy(landed, landed, rsem.at[t]).wait()
            arrived = recv[t].reshape(N * ROWS, M)
            if t == 0:
                pick = ones_where(iota((16, M), 1) == iota((16, M), 0) * R)
                numbers = dot_t(pick, arrived)
                col = iota((1, N * ROWS), 1) % ROWS
                numbers = jnp.concatenate([numbers[:, 2:], numbers[:, :2]], axis=1)
                pieces = []
                for q in range(4):
                    number = jnp.where((col == 4) | (col == 5), numbers[q : q + 1], -1.0)
                    pieces.append(ones_where(iota((CL, 1), 0).astype(F32) == number))
                big[pl.ds(FAR, 64), :] = jnp.concatenate(pieces, axis=0)
            got = dot(big[...], arrived)
            rows = recv[0].astype(F32)
            rows = jnp.concatenate([rows[:, 6, :], rows[:, 7, :]], axis=0).astype(BF16)
            numbers = dot(repeat4[...], rows)
            spread = ones_where(iota((M, M), 0) == iota((M, M), 1) // CL * R)
            numbers = dot(numbers.astype(BF16), spread)
            hot = jnp.where((iota((1, M), 1) % CL).astype(F32) == numbers, 1.0, 0.0)
            hot = jnp.where(iota((1, M), 1) < 64, hot, 0.0)
            pick4[...] = jnp.where(row4 < 2, hot, 0.0).astype(BF16)
            big4[pl.ds(FAR, 64), :] = jnp.transpose(jnp.where(row4 >= 2, hot, 0.0))[0:64, :].astype(BF16)
        else:
            landed = recv4.at[t - SHORT, pl.ds(0, N - 1)]
            pltpu.make_async_copy(landed, landed, rsem.at[t]).wait()
            got = dot(big4[...], recv4[t - SHORT].reshape(N * 4, M))
            landed = sum_b.at[t - SHORT, pl.ds(1, 7)]
            pltpu.make_async_copy(landed, landed, tree_r.at[t - SHORT, 1]).wait()
            totals = jnp.sum(sum_b[t - SHORT], axis=0)
            rw, ww = totals[:, 0:1], totals[:, 1:2]
        c4s[...] = copies(got[0:FAR] * (gmask if t < SHORT else jmask)[...]).astype(BF16)
        if t == 0:
            z = jnp.zeros((CL, R * R), F32)
            for i in range(4):
                part = pl.ds(i * 128, 128)
                c4 = c4s[part, :].astype(F32)
                hi, lo = split(coup[part, :].astype(F32) * jnp.concatenate([c4] * 8, axis=1))
                rows = hrow_t[:, i * 128 : (i + 1) * 128]
                z = z + dot(jnp.concatenate([rows, rows], axis=1), jnp.concatenate([hi, lo], axis=0))
        else:
            z = dot(hrow_t[...], coup[...] * jnp.concatenate([c4s[...]] * 8, axis=1))
        hi, lo = split(z)
        farsum = dot(jnp.concatenate([hi, lo], axis=0), e2_t[...])
        farsum = farsum[0:CL] + farsum[CL:]
        slots = jnp.zeros((CL, M), F32)
        for q in range(4):
            slots = slots + jnp.where(lane // R == q, got[FAR + 16 * q : FAR + 16 * (q + 1), :], 0.0)
        farsum = farsum + copies(slots)
        diag_far = jnp.where(own, jnp.concatenate([farsum] * 4, axis=1), 0.0).astype(BF16)
        product = product + dot(diag_far, basis_ref[...])

        spill_prev.wait_recv()
        spill_next.wait_recv()
        product = product + spin[t, 0] + spin[t, 1]

        if t == 0:
            image = product
        else:
            step = rw / (ww + EPS)
            solution = solution + step * residual
            residual = residual - step * image
            image = image - step * product
        field = image
        if t + 1 < ITERS:
            rw, ww = whole(residual * image), whole(image * image)

    rw, ww = whole(residual * image), whole(image * image)
    last_out[...] = jnp.where(lane == 0, rw, jnp.where(lane == 1, ww, 0.0))
    last_in[me] = last_out[...]

    for there in others:
        pltpu.make_async_remote_copy(
            last_out, last_in.at[me], lsem_s, lsem_r, device_id=there, device_id_type=LOGICAL
        ).start()
    for t in range(ITERS - SHORT):
        sent = sum_a.at[t, pl.ds(1, 15)]
        pltpu.make_async_copy(sent, sent, tree_s.at[t, 0]).wait()
        sent = sum_b.at[t, pl.ds(1, 7)]
        pltpu.make_async_copy(sent, sent, tree_s.at[t, 1]).wait()
    for t in range(ITERS):
        sent = send.at[t, pl.ds(0, N - 1)] if t < SHORT else send4.at[t - SHORT, pl.ds(0, N - 1)]
        pltpu.make_async_copy(sent, sent, ssem.at[t]).wait()
        for i in range(2):
            pltpu.make_async_copy(win.at[t, 1], win.at[t, 1], wsem_s.at[t, i]).wait()
            pltpu.make_async_copy(spout.at[t, i], spout.at[t, i], psem_s.at[t, i]).wait()
    everyone = last_in.at[pl.ds(0, N - 1)]
    pltpu.make_async_copy(everyone, everyone, lsem_r).wait()
    totals = jnp.sum(last_in[...], axis=0)
    step = totals[:, 0:1] / (totals[:, 1:2] + EPS)
    out_ref[0] = solution
    out_ref[1] = residual
    out_ref[2] = image
    out_ref[3] = jnp.broadcast_to(step, (CL, M))

    pltpu.make_async_copy(everyone, everyone, lsem_s).wait()


def on_device(rs, diag, near, nrow, ncol, ncount, basis, coup, frow, fcol, frank):
    vmem = pl.BlockSpec(memory_space=pltpu.VMEM)
    hbm = pl.BlockSpec(memory_space=pl.ANY)
    ints = jnp.int32
    v = pltpu.VMEM
    dma = pltpu.SemaphoreType.DMA
    out = pl.pallas_call(
        kernel,
        out_shape=jax.ShapeDtypeStruct((4, CL, M), F32),
        in_specs=[hbm] * 12,
        out_specs=vmem,
        scratch_shapes=[
            v((CL, M), F32),
            v((CL, M), F32),
            v((1, NEAR), ints),
            v((1, NEAR), ints),
            pltpu.SMEM((1, 1), ints),
            v((CL * R, M), BF16),
            v((1, FAR), ints),
            v((1, FAR), ints),
            v((1, FAR), ints),
            v((8, N * (ROWS + 4)), ints),
            v((NEAR, M, M), BF16),
            v((FAR, R * R), BF16),
            v((FAR, R * R), BF16),
            v((FAR + 64, N * ROWS), BF16),
            v((N * ROWS, FAR), BF16),
            v((R * R, M), BF16),
            v((M, CL * R), BF16),
            v((FAR, CL), BF16),
            v((CL, FAR), BF16),
            v((FAR, M), F32),
            v((FAR, M), F32),
            v((NEAR, CL), BF16),
            v((NEAR, 3 * CL), BF16),
            v((CL, NEAR), BF16),
            v((3 * CL, NEAR), BF16),
            v((FAR, M), BF16),
            v((FAR + 64, N * 4), BF16),
            v((N * 4, FAR), BF16),
            v((N * 4, M), BF16),
            v((N * 4, 2 * N), BF16),
            v((ITERS - SHORT, N, 4, M), BF16),
            v((ITERS - SHORT, N, 4, M), BF16),
            v((ITERS - SHORT, 1, M), F32),
            v((ITERS - SHORT, 16, 1, M), F32),
            v((ITERS - SHORT, 1, M), F32),
            v((ITERS - SHORT, 8, 1, M), F32),
            dma((ITERS - SHORT, 2)),
            dma((ITERS - SHORT, 2)),
            v((NEAR, 2 * M), BF16),
            v((NEAR, 2 * M), BF16),
            v((NEAR, M), F32),
            v((NEAR, M), F32),
            v((FAR, M), BF16),
            v((SHORT, N, ROWS, M), BF16),
            v((SHORT, N, ROWS, M), BF16),
            v((ITERS, 3, CL, M), BF16),
            v((ITERS, 2, CL, M), F32),
            v((ITERS, 2, CL, M), F32),
            v((1, M), F32),
            v((N, 1, M), F32),
            dma((12,)),
            dma((ITERS,)),
            dma((ITERS,)),
            dma((ITERS, 2)),
            dma((ITERS, 2)),
            dma((ITERS, 2)),
            dma((ITERS, 2)),
            dma,
            dma,
        ],
        compiler_params=pltpu.CompilerParams(
            collective_id=0, has_side_effects=True, vmem_limit_bytes=60 << 20
        ),
    )(
        rs,
        diag,
        near,
        nrow.reshape(1, NEAR),
        ncol.reshape(1, NEAR),
        ncount.reshape(1, 1),
        basis.reshape(CL * R, M),
        coup,
        frow.reshape(1, FAR),
        fcol.reshape(1, FAR),
        frank.reshape(1, FAR),
        jnp.asarray(order_table()),
    )
    return out[0] + out[3] * out[1], out[1] - out[3] * out[2]


def solution(mesh):
    flat = P(AXES)
    two = P(AXES, None)
    three = P(AXES, None, None)
    return jax.shard_map(
        on_device,
        mesh=mesh,
        in_specs=(two, two, three, flat, flat, flat, three, two, flat, flat, flat),
        out_specs=(two, two),
        check_vma=False,
    )
```
